32 devices in a mesh: rep: 4 (over y, x), fsdp: 8 (over z, core).
Axes of the slice: x: 2, y: 2, z: 4, core: 2. Of those that a mesh axis runs over, the one named last changes fastest.
Arguments:
- tokens: bfloat16 [49152, 576], P(('rep', 'fsdp')), may hold values from -6 to 6
- segment: int32 [49152], P(('rep', 'fsdp')), may hold values from -1 to 767, as said below
- attn_gain: bfloat16 [2, 576], P(None, 'fsdp'), may hold values from 0.099609375 to 1.8984375
- w_query: bfloat16 [2, 576, 576], P(None, 'fsdp'), may hold values from -0.25 to 0.25
- key_weight: bfloat16 [2, 576, 192], P(None, 'fsdp'), may hold values from -0.25 to 0.25
- value_weight: bfloat16 [2, 576, 192], P(None, 'fsdp'), may hold values from -0.25 to 0.25
- w_out: bfloat16 [2, 576, 576], P(None, 'fsdp'), may hold values from -3 to 3
- mlp_gain: bfloat16 [2, 576], P(None, 'fsdp'), may hold values from 0.099609375 to 1.8984375
- gate_weight: bfloat16 [2, 576, 1536], P(None, 'fsdp'), may hold values from -0.25 to 0.25
- up_weight: bfloat16 [2, 576, 1536], P(None, 'fsdp'), may hold values from -0.25 to 0.25
- down_weight: bfloat16 [2, 1536, 576], P(None, 'fsdp'), may hold values from -0.15625 to 0.15625
- cotangent: bfloat16 [49152, 576], P(('rep', 'fsdp')), may hold values from -6 to 6
Outputs:
- out_tokens: bfloat16 [49152, 576], P(('rep', 'fsdp'))
- grad_tokens: float32 [49152, 576], P(('rep', 'fsdp'))
- grad_attn_gain: float32 [2, 576], P(None, 'fsdp')
- grad_query: float32 [2, 576, 576], P(None, 'fsdp')
- grad_key: float32 [2, 576, 192], P(None, 'fsdp')
- grad_value: float32 [2, 576, 192], P(None, 'fsdp')
- grad_out: float32 [2, 576, 576], P(None, 'fsdp')
- grad_mlp_gain: float32 [2, 576], P(None, 'fsdp')
- grad_gate: float32 [2, 576, 1536], P(None, 'fsdp')
- grad_up: float32 [2, 576, 1536], P(None, 'fsdp')
- grad_down: float32 [2, 1536, 576], P(None, 'fsdp')
The draws below stay inside these ranges and needn't reach their ends.
Inputs may be any that keep to these rules, and one draw needn't show every extreme that they name: `segment`: each aligned block of 768 rows (one micro-batch of one device) holds whole sequences numbered 0, 1, 2, ... in order, then padding rows marked -1; no sequence has more than 512 rows and one has exactly 512; some block has no padding; some block holds 768 sequences of one row each.
All inputs are finite; a program needn't handle non-finite values.
Results may differ from the reference program's by a relative error of at most 0.025.
Values may be sent and summed in bfloat16 or wider, within the bound.
A program may use at most 384 MiB of HBM per device.

```python
import jax
import jax.numpy as jnp
from jax import lax

MODEL_WIDTH = 576
QUERY_HEADS = 9
KEY_VALUE_HEADS = 3
HEAD_WIDTH = 64
FF = 1536
DECODER_LAYERS = 2
MICRO = 2
SEQ_MAX = 512
MB_ROWS = 768
TOK_DEV = 1536
TOKENS = 49152


def draw_segment(key, part):
    blocks = TOKENS // MB_ROWS
    subkeys = jax.random.split(key, 3)
    row_index = jnp.arange(MB_ROWS, dtype=jnp.int32)
    block_index = jnp.arange(blocks, dtype=jnp.int32)[:, None]
    boundary = jax.random.randint(subkeys[0], (blocks, MB_ROWS), 0, SEQ_MAX) < 3
    full_block = jax.random.randint(subkeys[1], (), 0, blocks)
    single_block = (full_block + 1) % blocks
    full_rows = block_index == full_block
    single_rows = block_index == single_block
    boundary = jnp.where(full_rows & (row_index[None, :] < SEQ_MAX), False, boundary)
    boundary = boundary | (row_index % SEQ_MAX == 0)[None, :]
    boundary = boundary | single_rows
    live_count = jax.random.randint(subkeys[2], (blocks, 1), MB_ROWS // 4, MB_ROWS + 1)
    live_count = jnp.where(full_rows | single_rows, MB_ROWS, live_count)
    numbers = jnp.cumsum(boundary.astype(jnp.int32), axis=1) - 1
    numbers = jnp.where(row_index[None, :] < live_count, numbers, -1)
    return numbers.reshape(TOKENS).astype(jnp.int32)


def block_levels(rng, dims, shards, smallest, high):
    level = 1.0
    for dim, parts in shards:
        draws = jax.random.uniform(jax.random.fold_in(jax.random.fold_in(rng, 6), dim), (parts,), jnp.float32, smallest / len(shards), high / len(shards))
        level = level * jnp.repeat(jnp.exp(draws), dims[dim] // parts).reshape((-1,) + (1,) * (len(dims) - 1 - dim))
    return level


def scatter_about(stream_key, extent, scale, bound, pieces=(), held_as=jnp.bfloat16):
    entries = jax.random.normal(stream_key, extent, jnp.float32) * scale
    if len(pieces) > 0:
        entries = block_levels(stream_key, extent, pieces, -0.22, 0.18) * entries
    return jnp.clip(entries, min=-bound, max=bound).astype(held_as)


def setup_inputs(seed: int = 0) -> dict:
    key_of = jax.random.split(jax.random.key(seed), 13)
    return {
        "tokens": scatter_about(key_of[0], (TOKENS, MODEL_WIDTH), 1.0, 6.0, ((0, 32),)),
        "segment": draw_segment(jax.random.fold_in(key_of[12], 71), 0),
        "attn_gain": jnp.clip(1.0 + 0.18 * jax.random.normal(key_of[2], (DECODER_LAYERS, MODEL_WIDTH), jnp.float32), 0.099609375, 1.8984375).astype(jnp.bfloat16),
        "w_query": scatter_about(key_of[3], (DECODER_LAYERS, MODEL_WIDTH, QUERY_HEADS * HEAD_WIDTH), MODEL_WIDTH ** -0.5, 0.25, ((1, 8),)),
        "key_weight": scatter_about(key_of[4], (DECODER_LAYERS, MODEL_WIDTH, KEY_VALUE_HEADS * HEAD_WIDTH), MODEL_WIDTH ** -0.5, 0.25, ((1, 8),)),
        "value_weight": scatter_about(key_of[5], (DECODER_LAYERS, MODEL_WIDTH, KEY_VALUE_HEADS * HEAD_WIDTH), MODEL_WIDTH ** -0.5, 0.25, ((1, 8),)),
        "w_out": scatter_about(key_of[6], (DECODER_LAYERS, QUERY_HEADS * HEAD_WIDTH, MODEL_WIDTH), (max(QUERY_HEADS * HEAD_WIDTH * 4 // SEQ_MAX, 4)) ** -0.5, 3.0, ((1, 8),)),
        "mlp_gain": jnp.clip(1.0 + 0.18 * jax.random.normal(key_of[7], (DECODER_LAYERS, MODEL_WIDTH), jnp.float32), 0.099609375, 1.8984375).astype(jnp.bfloat16),
        "gate_weight": scatter_about(key_of[8], (DECODER_LAYERS, MODEL_WIDTH, FF), MODEL_WIDTH ** -0.5, 0.25, ((1, 8),)),
        "up_weight": scatter_about(key_of[9], (DECODER_LAYERS, MODEL_WIDTH, FF), MODEL_WIDTH ** -0.5, 0.25, ((1, 8),)),
        "down_weight": scatter_about(key_of[10], (DECODER_LAYERS, FF, MODEL_WIDTH), FF ** -0.5, 0.15625, ((1, 8),)),
        "cotangent": scatter_about(key_of[11], (TOKENS, MODEL_WIDTH), 1.0, 6.0, ((0, 32),)),
    }


@jax.custom_vjp
def lower_precision(v):
    return lax.optimization_barrier(v.astype(jnp.bfloat16)).astype(jnp.float32)

@jax.custom_vjp
def lower_precision_back(v):
    return v

def low_keep(v):
    return (lower_precision(v), None)

def low_pass(kept, grad):
    return (grad,)

def back_keep(v):
    return (v, None)

def back_low(kept, grad):
    return (lower_precision(grad),)
lower_precision.defvjp(low_keep, low_pass)
lower_precision_back.defvjp(back_keep, back_low)
epsilon = 1e-05
rope_base = 100000.0
masked_fill = -1e+30
highest_precision = lax.Precision.HIGHEST

def geometry(segment):
    count_of_rows = segment.shape[-1]
    row_index = jnp.arange(count_of_rows, dtype=jnp.int32)
    same_segment = segment[..., :, None] == segment[..., None, :]
    earlier = row_index[None, :] < row_index[:, None]
    position = lax.optimization_barrier(jnp.sum(jnp.where(same_segment & earlier, 1, 0).astype(jnp.int32), axis=-1))
    allowed = same_segment & (row_index[None, :] <= row_index[:, None])
    active_rows = jnp.where(segment >= 0, 1.0, 0.0).astype(jnp.float32)[..., None]
    frequency = rope_base ** (-2.0 * jnp.arange(HEAD_WIDTH // 2, dtype=jnp.float32) / HEAD_WIDTH)
    angles = position.astype(jnp.float32)[..., None] * frequency
    return (allowed, active_rows, jnp.cos(angles)[..., None, :], jnp.sin(angles)[..., None, :])

def rotary_apply(vectors, cosine_table, sine_values):
    half_width = vectors.shape[-1] // 2
    first_half = vectors[..., :half_width]
    second_half = vectors[..., half_width:]
    return jnp.concatenate([first_half * cosine_table - second_half * sine_values, second_half * cosine_table + first_half * sine_values], axis=-1)

def norm_apply(value_rows, gain_row):
    factor = lax.rsqrt(lax.optimization_barrier(jnp.mean(value_rows * value_rows, axis=-1, keepdims=True)) + epsilon)
    return value_rows * factor * gain_row

def layer_apply(residual, params, layout):
    attn_gain, w_query, key_weight, value_weight, w_out, mlp_gain, gate_weight, up_weight, down_weight = params
    allowed, active_rows, cosine_table, sine_values = layout
    leading_block = residual.shape[:-1]
    scale = HEAD_WIDTH ** (-0.5)
    normed = lower_precision(norm_apply(residual, attn_gain))
    query_rows = lower_precision_back(jnp.einsum('mrd,de->mre', normed, w_query, precision=highest_precision))
    key_rows = lower_precision_back(jnp.einsum('mrd,de->mre', normed, key_weight, precision=highest_precision))
    value_rows = lower_precision_back(jnp.einsum('mrd,de->mre', normed, value_weight, precision=highest_precision))
    query_rows = lower_precision(rotary_apply(query_rows.reshape(leading_block + (QUERY_HEADS, HEAD_WIDTH)), cosine_table, sine_values))
    key_rows = lower_precision(rotary_apply(key_rows.reshape(leading_block + (KEY_VALUE_HEADS, HEAD_WIDTH)), cosine_table, sine_values))
    value_rows = lower_precision(value_rows).reshape(leading_block + (KEY_VALUE_HEADS, HEAD_WIDTH))
    grouped_heads = query_rows.reshape(leading_block + (KEY_VALUE_HEADS, QUERY_HEADS // KEY_VALUE_HEADS, HEAD_WIDTH))
    scores = lower_precision_back(jnp.einsum('mqgjd,mkgd->mgjqk', grouped_heads, key_rows, precision=highest_precision) * scale)
    masked = jnp.where(allowed[:, None, None], scores, masked_fill)
    probs = lower_precision(jax.nn.softmax(masked, axis=-1))
    mixed = jnp.einsum('mgjqk,mkgd->mqgjd', probs, value_rows, precision=highest_precision).reshape(leading_block + (QUERY_HEADS * HEAD_WIDTH,))
    mixed = lower_precision(lower_precision_back(mixed))
    hidden_state = residual + lower_precision_back(jnp.einsum('mre,ed->mrd', mixed, w_out, precision=highest_precision)) * active_rows
    normed_feed_input = lower_precision(norm_apply(hidden_state, mlp_gain))
    gate_branch = lower_precision_back(jnp.einsum('hwl,la->hwa', normed_feed_input, gate_weight, precision=highest_precision))
    up_branch = lower_precision_back(jnp.einsum('hwl,la->hwa', normed_feed_input, up_weight, precision=highest_precision))
    inner_product = lower_precision(lower_precision_back(jax.nn.silu(gate_branch) * up_branch))
    return hidden_state + lower_precision_back(jnp.einsum('ews,sn->ewn', inner_product, down_weight, precision=highest_precision)) * active_rows

def reference(tokens, segment, attn_gain, w_query, key_weight, value_weight, w_out, mlp_gain, gate_weight, up_weight, down_weight, cotangent):
    groups = TOKENS // TOK_DEV
    weights = tuple((item.astype(jnp.float32) for item in (attn_gain, w_query, key_weight, value_weight, w_out, mlp_gain, gate_weight, up_weight, down_weight)))
    seg_groups = segment.reshape(groups, MICRO, MB_ROWS)

    def forward(residual, params):

        def one_group(paired):
            value_rows, seg_rows = paired
            layout = geometry(seg_rows)
            for layer_index in range(DECODER_LAYERS):
                value_rows = layer_apply(value_rows, tuple((weight[layer_index] for weight in params)), layout)
            return value_rows
        result = lax.map(jax.checkpoint(one_group), (residual.reshape(groups, MICRO, MB_ROWS, MODEL_WIDTH), seg_groups))
        return result.reshape(TOKENS, MODEL_WIDTH)
    result, pullback = jax.vjp(forward, tokens.astype(jnp.float32), weights)
    grad_input, grad_params = pullback(cotangent.astype(jnp.float32))
    return (result.astype(jnp.bfloat16), grad_input, grad_params[0], grad_params[1], grad_params[2], grad_params[3], grad_params[4], grad_params[5], grad_params[6], grad_params[7], grad_params[8])
```

```python
import functools

import jax
import jax.numpy as jnp
from jax import lax
from jax.experimental import pallas as pl
from jax.experimental.pallas import tpu as pltpu
from jax.sharding import PartitionSpec as P

QUERY_HEADS = 9
KEY_VALUE_HEADS = 3
HEAD_WIDTH = 64
DECODER_LAYERS = 2
MICRO = 2
GROUP = QUERY_HEADS // KEY_VALUE_HEADS
Q_WIDTH = QUERY_HEADS * HEAD_WIDTH
KV_WIDTH = KEY_VALUE_HEADS * HEAD_WIDTH
QK_WIDTH = Q_WIDTH + KV_WIDTH
LSE_ROWS = 16
SCALE = HEAD_WIDTH ** (-0.5)

epsilon = 1e-05
rope_base = 100000.0
masked_fill = -1e30
f32 = jnp.float32
bf16 = jnp.bfloat16


def nn(left, right):
    return jnp.dot(left, right, preferred_element_type=f32)


def nt(left, right):
    return lax.dot_general(left, right, (((1,), (1,)), ((), ())), preferred_element_type=f32)


def tn(left, right):
    return lax.dot_general(left, right, (((0,), (0,)), ((), ())), preferred_element_type=f32)


def geometry(segment):
    size = segment.shape[0] // MICRO
    seg = segment.reshape(MICRO, size)
    index = jnp.arange(size, dtype=jnp.int32)
    same = seg[:, :, None] == seg[:, None, :]
    earlier = index[None, :] < index[:, None]
    position = jnp.sum(jnp.where(same & earlier, 1, 0).astype(jnp.int32), axis=-1)
    frequency = rope_base ** (-2.0 * jnp.arange(HEAD_WIDTH // 2, dtype=f32) / HEAD_WIDTH)
    angles = position.reshape(-1).astype(f32)[:, None] * frequency
    cosine, sine = jnp.cos(angles), jnp.sin(angles)
    table = jnp.concatenate([cosine] * 4 + [-sine, sine] * 2, axis=1)
    live = jnp.where(segment >= 0, 1.0, 0.0).astype(f32)[:, None]
    return live, table


def swap_halves(rows):
    lane = lax.broadcasted_iota(jnp.int32, rows.shape, 1)
    first = (lane % HEAD_WIDTH) < HEAD_WIDTH // 2
    return jnp.where(
        first, pltpu.roll(rows, 128 - HEAD_WIDTH // 2, 1), pltpu.roll(rows, HEAD_WIDTH // 2, 1)
    )


def rotate(rows, cosine, sine):
    parts = []
    for first in range(0, rows.shape[1], 128):
        slab = rows[:, first : first + 128]
        parts.append(slab * cosine + swap_halves(slab) * sine)
    return jnp.concatenate(parts, axis=1)


def tile_of(rows):
    return 256 if rows % 256 == 0 else rows


def heads_stacked(ref, start, size, group):
    first = group * GROUP * HEAD_WIDTH
    piece = ref[start : start + size, first : first + GROUP * HEAD_WIDTH]
    return jnp.concatenate(
        [piece[:, j * HEAD_WIDTH : (j + 1) * HEAD_WIDTH] for j in range(GROUP)], axis=0
    )


def heads_split(stacked, size):
    turned = stacked.T
    return [turned[j * size : (j + 1) * size] for j in range(GROUP)]


def mask_bias(column_ref, row_ref, start, size):
    reach = start + size
    shape = (reach, size)
    key = lax.broadcasted_iota(jnp.int32, shape, 0)
    query = lax.broadcasted_iota(jnp.int32, shape, 1) + start
    same = column_ref[:reach, :] == row_ref[0, :, start:reach]
    bias = jnp.where(same & (key <= query), 0.0, masked_fill)
    return jnp.concatenate([bias] * GROUP, axis=1)


def norm(rows):
    return lax.rsqrt(jnp.mean(rows * rows, axis=-1, keepdims=True) + epsilon)


def row_line(ref, start, size, group):
    return jnp.concatenate(
        [ref[group * GROUP + j : group * GROUP + j + 1, start : start + size] for j in range(GROUP)],
        axis=1,
    )


def attn_forward_kernel(
    x_ref, column_ref, row_ref, live_ref, table_ref, gain_ref, weight_ref,
    h_ref, qk_ref, v_ref, a_ref, lse_ref,
):
    rows = x_ref.shape[0]
    x = x_ref[...].astype(f32)
    normed = (x * norm(x) * gain_ref[...]).astype(bf16)
    qk = nn(normed, weight_ref[:, :QK_WIDTH])
    v_ref[...] = nn(normed, weight_ref[:, QK_WIDTH + Q_WIDTH :]).astype(bf16)
    qk = rotate(qk, table_ref[:, :128], table_ref[:, 128:]).astype(bf16)
    qk_ref[:, :Q_WIDTH] = qk[:, :Q_WIDTH] * SCALE
    qk_ref[:, Q_WIDTH:] = qk[:, Q_WIDTH:]
    size = tile_of(rows)
    for start in range(0, rows, size):
        reach = start + size
        bias = mask_bias(column_ref, row_ref, start, size)
        outputs = []
        for group in range(KEY_VALUE_HEADS):
            lanes = slice(group * HEAD_WIDTH, (group + 1) * HEAD_WIDTH)
            klanes = slice(Q_WIDTH + group * HEAD_WIDTH, Q_WIDTH + (group + 1) * HEAD_WIDTH)
            queries = heads_stacked(qk_ref, start, size, group)
            scores = nt(qk_ref[:reach, klanes], queries) + bias
            peak = jnp.max(scores, axis=0, keepdims=True)
            expo = jnp.exp(scores - peak)
            total = jnp.sum(expo, axis=0, keepdims=True)
            mixed = tn(v_ref[:reach, lanes], expo.astype(bf16)) * (1.0 / total)
            outputs += heads_split(mixed, size)
            line = peak + jnp.log(total)
            for j in range(GROUP):
                lse_ref[group * GROUP + j : group * GROUP + j + 1, start:reach] = line[
                    :, j * size : (j + 1) * size
                ]
        a_ref[start:reach, :] = jnp.concatenate(outputs, axis=1).astype(bf16)
    out = nn(a_ref[...], weight_ref[:, QK_WIDTH : QK_WIDTH + Q_WIDTH])
    h_ref[...] = x_ref[...].astype(f32) + out * live_ref[...]


def attn_backward_kernel(
    x_ref, dh_ref, column_ref, row_ref, live_ref, table_ref, gain_ref, weight_ref,
    qk_ref, v_ref, a_ref, lse_ref,
    dx_ref, grad_ref, gain_grad_ref,
    n1t_ref, at_ref, c_ref, dqk_ref, dv_ref, da_ref, weight_line_ref, dqk_sum, dv_sum,
):
    step = pl.program_id(0)
    rows = x_ref.shape[0]
    here = pl.ds(pl.multiple_of(step * rows, rows), rows)
    c = (dh_ref[...] * live_ref[...]).astype(bf16)
    c_ref[here, :] = c
    da = nt(c, weight_ref[:, QK_WIDTH : QK_WIDTH + Q_WIDTH]).astype(bf16)
    da_ref[...] = da
    a = a_ref[...]
    at_ref[:, here] = a.T
    product = da.astype(f32) * a.astype(f32)
    high = product.astype(bf16)
    low = (product - high.astype(f32)).astype(bf16)
    pick = (
        lax.broadcasted_iota(jnp.int32, (LSE_ROWS, Q_WIDTH), 1) // HEAD_WIDTH
        == lax.broadcasted_iota(jnp.int32, (LSE_ROWS, Q_WIDTH), 0)
    )
    pick = jnp.where(pick, 1.0, 0.0).astype(bf16)
    weight_line_ref[...] = nt(pick, high) + nt(pick, low)
    size = tile_of(rows)
    for start in reversed(range(0, rows, size)):
        reach = start + size
        bias = mask_bias(column_ref, row_ref, start, size)
        query_grads = []
        for group in range(KEY_VALUE_HEADS):
            lanes = slice(group * HEAD_WIDTH, (group + 1) * HEAD_WIDTH)
            klanes = slice(Q_WIDTH + group * HEAD_WIDTH, Q_WIDTH + (group + 1) * HEAD_WIDTH)
            queries = heads_stacked(qk_ref, start, size, group)
            upstream = heads_stacked(da_ref, start, size, group)
            keys = qk_ref[:reach, klanes]
            values = v_ref[:reach, lanes]
            probs = jnp.exp(nt(keys, queries) + bias - row_line(lse_ref, start, size, group))
            value_grad = nn(probs.astype(bf16), upstream)
            grad_probs = nt(values, upstream)
            grad_scores = (
                probs * (grad_probs - row_line(weight_line_ref, start, size, group))
            ).astype(bf16)
            key_grad = nn(grad_scores, queries)
            query_grads += heads_split(tn(keys, grad_scores) * SCALE, size)
            if reach == rows:
                dqk_sum[:, klanes] = key_grad
                dv_sum[:, lanes] = value_grad
            else:
                dqk_sum[:reach, klanes] += key_grad
                dv_sum[:reach, lanes] += value_grad
        dqk_sum[start:reach, :Q_WIDTH] = jnp.concatenate(query_grads, axis=1)
    dqk = rotate(dqk_sum[...], table_ref[:, :128], -table_ref[:, 128:]).astype(bf16)
    dqk_ref[here, :] = dqk
    dv = dv_sum[...].astype(bf16)
    dv_ref[here, :] = dv
    dn = nt(dqk, weight_ref[:, :QK_WIDTH]) + nt(dv, weight_ref[:, QK_WIDTH + Q_WIDTH :])
    x = x_ref[...].astype(f32)
    factor = norm(x)
    unit = x * factor
    gain = gain_ref[...]
    n1t_ref[:, here] = (unit * gain).astype(bf16).T
    scaled = dn * gain
    dx_ref[...] = dh_ref[...] + factor * (
        scaled - unit * jnp.mean(scaled * unit, axis=-1, keepdims=True)
    )
    gain_part = jnp.sum(dn * unit, axis=0, keepdims=True)

    @pl.when(step == 0)
    def _():
        gain_grad_ref[...] = gain_part

    @pl.when(step > 0)
    def _():
        gain_grad_ref[...] += gain_part

    @pl.when(step == pl.num_programs(0) - 1)
    def _():
        grad_ref[:, :QK_WIDTH] = nn(n1t_ref[...], dqk_ref[...]).astype(bf16)
        grad_ref[:, QK_WIDTH : QK_WIDTH + Q_WIDTH] = nn(at_ref[...], c_ref[...]).astype(bf16)
        grad_ref[:, QK_WIDTH + Q_WIDTH :] = nn(n1t_ref[...], dv_ref[...]).astype(bf16)


def ff_forward_kernel(h_ref, live_ref, gain_ref, wg_ref, wu_ref, wd_ref, y_ref):
    h = h_ref[...]
    normed = (h * norm(h) * gain_ref[...]).astype(bf16)
    gate = nn(normed, wg_ref[...])
    up = nn(normed, wu_ref[...])
    half = 0.5 * gate
    inner = ((half + half * jnp.tanh(half)) * up).astype(bf16)
    y_ref[...] = h + nn(inner, wd_ref[...]) * live_ref[...]


def ff_backward_kernel(
    last, h_ref, dy_ref, live_ref, gain_ref, wg_ref, wu_ref, wd_ref, *rest,
):
    if last:
        y_ref, *rest = rest
    (dh_ref, gg_ref, gu_ref, gd_ref, gain_grad_ref, n2t_ref, et_ref, m_ref, dg_ref, du_ref) = rest
    step = pl.program_id(0)
    rows = h_ref.shape[0]
    here = pl.ds(pl.multiple_of(step * rows, rows), rows)
    h = h_ref[...]
    factor = norm(h)
    unit = h * factor
    gain = gain_ref[...]
    normed = (unit * gain).astype(bf16)
    n2t_ref[:, here] = normed.T
    live = live_ref[...]
    dy = dy_ref[...].astype(f32)
    e = (dy * live).astype(bf16)
    et_ref[:, here] = e.T
    gate = nn(normed, wg_ref[...])
    up = nn(normed, wu_ref[...])
    sig = 0.5 + 0.5 * jnp.tanh(0.5 * gate)
    silu = gate * sig
    inner = (silu * up).astype(bf16)
    m_ref[here, :] = inner
    dm = nt(e, wd_ref[...]).astype(bf16).astype(f32)
    dgate = (dm * up * (sig + silu * (1.0 - sig))).astype(bf16)
    dup = (dm * silu).astype(bf16)
    dg_ref[here, :] = dgate
    du_ref[here, :] = dup
    if last:
        y_ref[...] = (h + nn(inner, wd_ref[...]) * live).astype(bf16)
    dn = nt(dgate, wg_ref[...]) + nt(dup, wu_ref[...])
    scaled = dn * gain
    dh_ref[...] = dy + factor * (scaled - unit * jnp.mean(scaled * unit, axis=-1, keepdims=True))
    gain_part = jnp.sum(dn * unit, axis=0, keepdims=True)

    @pl.when(step == 0)
    def _():
        gain_grad_ref[...] = gain_part

    @pl.when(step > 0)
    def _():
        gain_grad_ref[...] += gain_part

    @pl.when(step == pl.num_programs(0) - 1)
    def _():
        ff = m_ref.shape[1]
        for first in range(0, ff, 512):
            cols = slice(first, first + 512)
            gg_ref[:, cols] = nn(n2t_ref[...], dg_ref[:, cols]).astype(bf16)
            gu_ref[:, cols] = nn(n2t_ref[...], du_ref[:, cols]).astype(bf16)
            gd_ref[cols, :] = nn(et_ref[...], m_ref[:, cols]).astype(bf16).T


def row_spec(size, width):
    return pl.BlockSpec((size, width), lambda i: (i, 0))


def whole_spec(shape):
    return pl.BlockSpec(shape, lambda i: (0,) * len(shape), pipeline_mode=pl.Buffered(1))


def still_spec(shape):
    return pl.BlockSpec(shape, lambda i: (0,) * len(shape))


def shape(dims, dtype):
    return jax.ShapeDtypeStruct(dims, dtype)


def params(mib=60):
    return pltpu.CompilerParams(vmem_limit_bytes=mib * 2**20, dimension_semantics=("arbitrary",))


def cost(flops, *arrays):
    return pl.CostEstimate(
        flops=int(flops),
        bytes_accessed=sum(int(a.size) * a.dtype.itemsize for a in arrays),
        transcendentals=0,
    )


def attn_forward(x, segment, live, table, gain, weight):
    total, width = x.shape
    size = total // MICRO
    outs = [
        shape((total, width), f32),
        shape((total, QK_WIDTH), bf16),
        shape((total, KV_WIDTH), bf16),
        shape((total, Q_WIDTH), bf16),
        shape((LSE_ROWS, total), f32),
    ]
    return pl.pallas_call(
        attn_forward_kernel,
        grid=(MICRO,),
        in_specs=[
            row_spec(size, width),
            row_spec(size, 1),
            pl.BlockSpec((1, 1, size), lambda i: (i, 0, 0)),
            row_spec(size, 1),
            row_spec(size, 256),
            whole_spec(gain.shape),
            whole_spec(weight.shape),
        ],
        out_specs=[row_spec(size, o.shape[1]) for o in outs[:4]]
        + [pl.BlockSpec((LSE_ROWS, size), lambda i: (0, i))],
        out_shape=outs,
        compiler_params=params(),
        cost_estimate=cost(2 * total * (width * 1536 + size * Q_WIDTH * 4), x, weight, *outs),
        name="attn_fwd",
    )(x, segment.reshape(-1, 1), segment.reshape(MICRO, 1, size), live, table, gain, weight)


def attn_backward(x, dh, segment, live, table, gain, weight, saved):
    total, width = x.shape
    size = total // MICRO
    qk, v, a, lse = saved
    outs = [shape((total, width), f32), shape(weight.shape, bf16), shape((1, width), f32)]
    return pl.pallas_call(
        attn_backward_kernel,
        grid=(MICRO,),
        in_specs=[
            row_spec(size, width),
            row_spec(size, width),
            row_spec(size, 1),
            pl.BlockSpec((1, 1, size), lambda i: (i, 0, 0)),
            row_spec(size, 1),
            row_spec(size, 256),
            whole_spec(gain.shape),
            whole_spec(weight.shape),
            row_spec(size, QK_WIDTH),
            row_spec(size, KV_WIDTH),
            row_spec(size, Q_WIDTH),
            pl.BlockSpec((LSE_ROWS, size), lambda i: (0, i)),
        ],
        out_specs=[row_spec(size, width), still_spec(weight.shape), still_spec((1, width))],
        out_shape=outs,
        scratch_shapes=[
            pltpu.VMEM((width, total), bf16),
            pltpu.VMEM((Q_WIDTH, total), bf16),
            pltpu.VMEM((total, width), bf16),
            pltpu.VMEM((total, QK_WIDTH), bf16),
            pltpu.VMEM((total, KV_WIDTH), bf16),
            pltpu.VMEM((size, Q_WIDTH), bf16),
            pltpu.VMEM((LSE_ROWS, size), f32),
            pltpu.VMEM((size, QK_WIDTH), f32),
            pltpu.VMEM((size, KV_WIDTH), f32),
        ],
        compiler_params=params(),
        cost_estimate=cost(2 * total * (width * 3072 + size * Q_WIDTH * 10), x, dh, weight, *outs),
        name="attn_bwd",
    )(
        x, dh, segment.reshape(-1, 1), segment.reshape(MICRO, 1, size), live, table, gain, weight,
        qk, v, a, lse,
    )


def ff_forward(h, live, gain, wg, wu, wd):
    total, width = h.shape
    size = tile_of(total)
    out = shape((total, width), f32)
    return pl.pallas_call(
        ff_forward_kernel,
        grid=(total // size,),
        in_specs=[row_spec(size, width), row_spec(size, 1), whole_spec(gain.shape)]
        + [whole_spec(w.shape) for w in (wg, wu, wd)],
        out_specs=row_spec(size, width),
        out_shape=out,
        compiler_params=params(),
        cost_estimate=cost(6 * total * wg.size, h, wg, wu, wd, out),
        name="ff_fwd",
    )(h, live, gain, wg, wu, wd)


def ff_backward(h, dy, live, gain, wg, wu, wd, last):
    total, width = h.shape
    ff = wg.shape[1]
    size = tile_of(total)
    outs = [
        shape((total, width), f32),
        shape(wg.shape, bf16),
        shape(wu.shape, bf16),
        shape(wd.shape, bf16),
        shape((1, width), f32),
    ]
    specs = [row_spec(size, width)] + [still_spec(o.shape) for o in outs[1:]]
    if last:
        outs = [shape((total, width), bf16)] + outs
        specs = [row_spec(size, width)] + specs
    return pl.pallas_call(
        functools.partial(ff_backward_kernel, last),
        grid=(total // size,),
        in_specs=[row_spec(size, width), row_spec(size, width), row_spec(size, 1)]
        + [whole_spec(gain.shape)]
        + [whole_spec(w.shape) for w in (wg, wu, wd)],
        out_specs=specs,
        out_shape=outs,
        scratch_shapes=[
            pltpu.VMEM((width, total), bf16),
            pltpu.VMEM((width, total), bf16),
            pltpu.VMEM((total, ff), bf16),
            pltpu.VMEM((total, ff), bf16),
            pltpu.VMEM((total, ff), bf16),
        ],
        compiler_params=params(),
        cost_estimate=cost(16 * total * wg.size, h, dy, wg, wu, wd, *outs),
        name="ff_bwd",
    )(h, dy, live, gain, wg, wu, wd)


def sum_shards(buffer):
    shard = lax.psum_scatter(buffer, "fsdp", scatter_dimension=0, tiled=False)
    return lax.psum(shard, "rep").astype(f32)


def local(
    tokens, segment, attn_gain, w_query, key_weight, value_weight, w_out, mlp_gain,
    gate_weight, up_weight, down_weight, cotangent,
):
    devices = lax.axis_size("fsdp")
    rows, ff = gate_weight.shape[1:]
    width = rows * devices
    down_rows = down_weight.shape[1]
    live, table = geometry(segment)

    gains = jnp.concatenate([attn_gain, mlp_gain]).reshape(1, 4 * rows)
    gains = jnp.pad(gains, ((0, 0), (0, QK_WIDTH + Q_WIDTH + KV_WIDTH - 4 * rows)))
    attn_w, feed_w = [], []
    for layer in range(DECODER_LAYERS):
        packed = jnp.concatenate(
            [w_query[layer], key_weight[layer], w_out[layer], value_weight[layer]], axis=1
        )
        if layer == 0:
            packed = jnp.concatenate([packed, gains])
            whole = lax.all_gather(packed, "fsdp", axis=0, tiled=False)
            all_gains = whole[:, rows, : 4 * rows].reshape(devices, 4, rows)
            all_gains = all_gains.transpose(1, 0, 2).reshape(4, 1, width).astype(f32)
            attn_w.append(whole[:, :rows].reshape(width, -1))
        else:
            attn_w.append(lax.all_gather(packed, "fsdp", axis=0, tiled=True))
        packed = jnp.concatenate(
            [gate_weight[layer], up_weight[layer], down_weight[layer].reshape(rows, ff)]
        )
        whole = lax.all_gather(packed, "fsdp", axis=0, tiled=False)
        feed_w.append(
            (
                whole[:, :rows].reshape(width, ff),
                whole[:, rows : 2 * rows].reshape(width, ff),
                whole[:, 2 * rows :].reshape(ff, width),
            )
        )

    h0, *kept0 = attn_forward(tokens, segment, live, table, all_gains[0], attn_w[0])
    x1 = ff_forward(h0, live, all_gains[2], *feed_w[0])
    h1, *kept1 = attn_forward(x1, segment, live, table, all_gains[1], attn_w[1])
    out_tokens, dh1, gg1, gu1, gd1, mg1 = ff_backward(
        h1, cotangent, live, all_gains[3], *feed_w[1], True
    )
    feed1 = sum_shards(
        jnp.concatenate(
            [g.reshape(devices, rows, ff) for g in (gg1, gu1, gd1)], axis=1
        )
    )
    dx1, ga1, ag1 = attn_backward(x1, dh1, segment, live, table, all_gains[1], attn_w[1], kept1)
    dh0, gg0, gu0, gd0, mg0 = ff_backward(h0, dx1, live, all_gains[2], *feed_w[0], False)
    feed0 = sum_shards(
        jnp.concatenate(
            [g.reshape(devices, rows, ff) for g in (gg0, gu0, gd0)], axis=1
        )
    )
    dx0, ga0, ag0 = attn_backward(
        tokens, dh0, segment, live, table, all_gains[0], attn_w[0], kept0
    )
    zero = jnp.zeros((devices, 1, ff - 4 * rows), bf16)
    gain_grads = jnp.concatenate(
        [g.reshape(devices, 1, rows).astype(bf16) for g in (ag0, ag1, mg0, mg1)] + [zero], axis=2
    )
    attn1 = sum_shards(ga1.reshape(devices, rows, ff))
    attn0 = sum_shards(jnp.concatenate([ga0.reshape(devices, rows, ff), gain_grads], axis=1))
    last = attn0[rows]
    attn = jnp.stack([attn0[:rows], attn1])
    feed = jnp.stack([feed0, feed1])
    return (
        out_tokens,
        dx0,
        last[: 2 * rows].reshape(2, rows),
        attn[:, :, :Q_WIDTH],
        attn[:, :, Q_WIDTH:QK_WIDTH],
        attn[:, :, QK_WIDTH + Q_WIDTH :],
        attn[:, :, QK_WIDTH : QK_WIDTH + Q_WIDTH],
        last[2 * rows : 4 * rows].reshape(2, rows),
        feed[:, :rows],
        feed[:, rows : 2 * rows],
        feed[:, 2 * rows :].reshape(2, down_rows, width),
    )


def solution(mesh):
    rows = P(("rep", "fsdp"), None)
    flat, cube = P(None, "fsdp"), P(None, "fsdp", None)
    in_specs = (rows, P(("rep", "fsdp")), flat, cube, cube, cube, cube, flat, cube, cube, cube, rows)
    out_specs = (rows, rows, flat, cube, cube, cube, cube, flat, cube, cube, cube)
    return jax.shard_map(local, mesh=mesh, in_specs=in_specs, out_specs=out_specs, check_vma=False)
```

```python
import functools

import jax
import jax.numpy as jnp
from jax import lax
from jax.experimental import pallas as pl
from jax.experimental.pallas import tpu as pltpu
from jax.sharding import PartitionSpec as P

QUERY_HEADS = 9
KEY_VALUE_HEADS = 3
HEAD_WIDTH = 64
DECODER_LAYERS = 2
MICRO = 2
GROUP = QUERY_HEADS // KEY_VALUE_HEADS
Q_WIDTH = QUERY_HEADS * HEAD_WIDTH
KV_WIDTH = KEY_VALUE_HEADS * HEAD_WIDTH
QK_WIDTH = Q_WIDTH + KV_WIDTH
LSE_ROWS = 16
SCALE = HEAD_WIDTH ** (-0.5)

epsilon = 1e-05
rope_base = 100000.0
masked_fill = -1e30
f32 = jnp.float32
bf16 = jnp.bfloat16


def nn(left, right):
    return jnp.dot(left, right, preferred_element_type=f32)


def nt(left, right):
    return lax.dot_general(left, right, (((1,), (1,)), ((), ())), preferred_element_type=f32)


def tn(left, right):
    return lax.dot_general(left, right, (((0,), (0,)), ((), ())), preferred_element_type=f32)


def geometry(segment):
    size = segment.shape[0] // MICRO
    seg = segment.reshape(MICRO, size)
    index = jnp.arange(size, dtype=jnp.int32)
    same = seg[:, :, None] == seg[:, None, :]
    earlier = index[None, :] < index[:, None]
    position = jnp.sum(jnp.where(same & earlier, 1, 0).astype(jnp.int32), axis=-1)
    frequency = rope_base ** (-2.0 * jnp.arange(HEAD_WIDTH // 2, dtype=f32) / HEAD_WIDTH)
    angles = position.reshape(-1).astype(f32)[:, None] * frequency
    cosine, sine = jnp.cos(angles), jnp.sin(angles)
    table = jnp.concatenate([cosine] * 4 + [-sine, sine] * 2, axis=1)
    live = jnp.where(segment >= 0, 1.0, 0.0).astype(f32)[:, None]
    return live, table


def swap_halves(rows):
    lane = lax.broadcasted_iota(jnp.int32, rows.shape, 1)
    first = (lane % HEAD_WIDTH) < HEAD_WIDTH // 2
    return jnp.where(
        first, pltpu.roll(rows, 128 - HEAD_WIDTH // 2, 1), pltpu.roll(rows, HEAD_WIDTH // 2, 1)
    )


def rotate(rows, cosine, sine):
    parts = []
    for first in range(0, rows.shape[1], 128):
        slab = rows[:, first : first + 128]
        parts.append(slab * cosine + swap_halves(slab) * sine)
    return jnp.concatenate(parts, axis=1)


def tile_of(rows):
    return 256 if rows % 256 == 0 else rows


def heads_stacked(ref, start, size, group):
    first = group * GROUP * HEAD_WIDTH
    piece = ref[start : start + size, first : first + GROUP * HEAD_WIDTH]
    return jnp.concatenate(
        [piece[:, j * HEAD_WIDTH : (j + 1) * HEAD_WIDTH] for j in range(GROUP)], axis=0
    )


def heads_split(stacked, size):
    turned = stacked.T
    return [turned[j * size : (j + 1) * size] for j in range(GROUP)]


def mask_bias(column_ref, row_ref, start, size):
    reach = start + size
    shape = (reach, size)
    key = lax.broadcasted_iota(jnp.int32, shape, 0)
    query = lax.broadcasted_iota(jnp.int32, shape, 1) + start
    same = column_ref[:reach, :] == row_ref[0, :, start:reach]
    bias = jnp.where(same & (key <= query), 0.0, masked_fill)
    return jnp.concatenate([bias] * GROUP, axis=1)


def norm(rows):
    return lax.rsqrt(jnp.mean(rows * rows, axis=-1, keepdims=True) + epsilon)


def row_line(ref, start, size, group):
    return jnp.concatenate(
        [ref[group * GROUP + j : group * GROUP + j + 1, start : start + size] for j in range(GROUP)],
        axis=1,
    )


MESH_AXES = ("rep", "fsdp")


class Place:
    def __init__(self):
        self.copies = lax.axis_size("rep")
        self.line = lax.axis_size("fsdp") // 2
        self.r = lax.axis_index("rep")
        index = lax.axis_index("fsdp")
        self.z = index // 2
        self.c = index % 2

    def at(self, r, z, c):
        return (r, 2 * z + c)

    def partner(self):
        return self.at(self.r, self.z, 1 - self.c)

    def chip(self, k):
        return lax.rem(self.z + k, self.line)

    def replica(self, j):
        return lax.rem(self.r + j, self.copies)

    def greet(self):
        barrier = pltpu.get_barrier_semaphore()
        peers = [self.partner()]
        peers += [self.at(self.r, self.chip(k), self.c) for k in range(1, self.line)]
        peers += [self.at(self.replica(j), self.z, self.c) for j in range(1, self.copies)]
        for peer in peers:
            pl.semaphore_signal(barrier, inc=1, device_id=peer, device_id_type=pl.DeviceIdType.MESH)
        pl.semaphore_wait(barrier, len(peers))


def remote(source, target, send, receive, device):
    return pltpu.make_async_remote_copy(
        src_ref=source, dst_ref=target, send_sem=send, recv_sem=receive,
        device_id=device, device_id_type=pl.DeviceIdType.MESH,
    )


def part_of(dims, parts):
    rows, cols = dims
    if cols % (128 * parts) == 0:
        return 1, cols // parts
    return 0, rows // parts


def can_cut(dims, parts):
    rows, cols = dims
    return cols % (128 * parts) == 0 or rows % (16 * parts) == 0


def piece(ref, lead, dims, parts, index):
    axis, size = part_of(dims, parts)
    if axis == 1:
        return ref.at[lead, :, pl.ds(pl.multiple_of(index * size, 128), size)]
    return ref.at[lead, pl.ds(pl.multiple_of(index * size, 16), size), :]


def piece_dims(dims, parts):
    axis, size = part_of(dims, parts)
    return (dims[0], size) if axis == 1 else (size, dims[1])


class Gather:
    def __init__(self, place, layer, shard, whole, sems):
        self.p, self.layer, self.shard, self.whole = place, layer, shard, whole
        self.sems = sems
        self.dims = shard.shape[1:]
        self.parts = place.copies

    @staticmethod
    def semaphores(copies, line):
        return [
            pltpu.SemaphoreType.DMA((2, line)),
            pltpu.SemaphoreType.DMA((2, line, copies)),
            pltpu.SemaphoreType.DMA((2, line)),
            pltpu.SemaphoreType.DMA,
        ]

    def own(self):
        p = self.p
        return pltpu.make_async_copy(
            self.shard.at[self.layer], self.whole.at[2 * p.z + p.c], self.sems[3]
        )

    def along(self, k):
        p = self.p
        return remote(
            piece(self.shard, self.layer, self.dims, self.parts, p.r),
            piece(self.whole, 2 * p.z + p.c, self.dims, self.parts, p.r),
            self.sems[0].at[0, k], self.sems[0].at[1, k], p.at(p.r, p.chip(k), p.c),
        )

    def across(self, k, j):
        p = self.p
        block = piece(
            self.whole, 2 * p.chip(p.line - k) + p.c, self.dims, self.parts, p.r
        )
        return remote(
            block, block, self.sems[1].at[0, k, j], self.sems[1].at[1, k, j],
            p.at(p.replica(j), p.z, p.c),
        )

    def pair(self, k):
        p = self.p
        index = 2 * p.chip(p.line - k) + p.c
        source = self.shard.at[self.layer] if k == 0 else self.whole.at[index]
        return remote(
            source, self.whole.at[index], self.sems[2].at[0, k], self.sems[2].at[1, k], p.partner()
        )

    def start(self):
        for k in range(1, self.p.line):
            self.along(k).start()
        self.own().start()
        self.pair(0).start()

    def second(self):
        for k in range(1, self.p.line):
            self.along(k).wait_recv()
            for j in range(1, self.p.copies):
                self.across(k, j).start()

    def third(self):
        for k in range(1, self.p.line):
            for j in range(1, self.p.copies):
                self.across(k, j).wait_recv()
            self.pair(k).start()

    def finish(self):
        self.own().wait()
        for k in range(self.p.line):
            self.pair(k).wait()
            if k:
                self.along(k).wait_send()
                for j in range(1, self.p.copies):
                    self.across(k, j).wait_send()


class Reduce:
    def __init__(self, place, source, out, buffers):
        self.p, self.source, self.out = place, source, out
        self.dims = source.shape[1:]
        self.parts = place.copies
        (self.mine, self.theirs, self.across_in, self.line_out, self.line_in, self.final,
         self.s0, self.s1, self.s2, self.s3, self.s4) = buffers

    @staticmethod
    def scratch(dims, copies, line):
        small = piece_dims(dims, copies)
        return [
            pltpu.VMEM((line,) + tuple(dims), bf16),
            pltpu.VMEM((line,) + tuple(dims), bf16),
            pltpu.VMEM((copies, line) + small, bf16),
            pltpu.VMEM((line,) + small, bf16),
            pltpu.VMEM((line,) + small, bf16),
            pltpu.VMEM((copies,) + small, bf16),
            pltpu.SemaphoreType.DMA((2, line)),
            pltpu.SemaphoreType.DMA((line,)),
            pltpu.SemaphoreType.DMA((2, copies, line)),
            pltpu.SemaphoreType.DMA((2, line)),
            pltpu.SemaphoreType.DMA((2, copies)),
        ]

    def pair(self, z):
        p = self.p
        return remote(
            self.source.at[2 * z + 1 - p.c], self.theirs.at[z],
            self.s0.at[0, z], self.s0.at[1, z], p.partner(),
        )

    def load(self, z):
        return pltpu.make_async_copy(
            self.source.at[2 * z + self.p.c], self.mine.at[z], self.s1.at[z]
        )

    def across(self, j, z):
        p = self.p
        return remote(
            piece(self.mine, z, self.dims, self.parts, p.replica(j)), self.across_in.at[j, z],
            self.s2.at[0, j, z], self.s2.at[1, j, z], p.at(p.replica(j), p.z, p.c),
        )

    def along(self, k):
        p = self.p
        return remote(
            self.line_out.at[p.chip(k)], self.line_in.at[k],
            self.s3.at[0, k], self.s3.at[1, k], p.at(p.r, p.chip(k), p.c),
        )

    def spread(self, j):
        p = self.p
        return remote(
            self.final.at[p.r], self.final.at[p.r],
            self.s4.at[0, j], self.s4.at[1, j], p.at(p.replica(j), p.z, p.c),
        )

    def start(self):
        for z in range(self.p.line):
            self.pair(z).start()
            self.load(z).start()

    def second(self):
        for z in range(self.p.line):
            self.load(z).wait()
            self.pair(z).wait_recv()
            self.mine[z] = (self.mine[z].astype(f32) + self.theirs[z].astype(f32)).astype(bf16)
            for j in range(1, self.p.copies):
                self.across(j, z).start()

    def third(self):
        for z in range(self.p.line):
            total = piece(self.mine, z, self.dims, self.parts, self.p.r)[...].astype(f32)
            for j in range(1, self.p.copies):
                self.across(j, z).wait_recv()
                total += self.across_in[j, z].astype(f32)
            self.line_out[z] = total.astype(bf16)
        for k in range(1, self.p.line):
            self.along(k).start()

    def fourth(self):
        total = self.line_out[self.p.z].astype(f32)
        for k in range(1, self.p.line):
            self.along(k).wait_recv()
            total += self.line_in[k].astype(f32)
        self.final[self.p.r] = total.astype(bf16)
        for j in range(1, self.p.copies):
            self.spread(j).start()

    def finish(self):
        for j in range(1, self.p.copies):
            self.spread(j).wait()
        axis, size = part_of(self.dims, self.parts)
        for index in range(self.parts):
            here = slice(index * size, (index + 1) * size)
            if axis == 1:
                self.out[:, here] = self.final[index].astype(f32)
            else:
                self.out[here, :] = self.final[index].astype(f32)
        for z in range(self.p.line):
            self.pair(z).wait_send()
            for j in range(1, self.p.copies):
                self.across(j, z).wait_send()
        for k in range(1, self.p.line):
            self.along(k).wait_send()


class Plan:
    def __init__(self, step, steps):
        self.step, self.steps, self.at = step, steps, {}

    def put(self, when, point, *acts):
        self.at.setdefault((when, point), []).extend(acts)

    def run(self, point):
        for when in range(self.steps):
            acts = self.at.get((when, point), [])
            if acts:
                @pl.when(self.step == when)
                def _(acts=acts):
                    for act in acts:
                        act()


def attn_forward_kernel(
    layer, count, turned, x_ref, column_ref, row_ref, live_ref, table_ref, gain_ref, weight_ref,
    *rest
):
    shards, rest = rest[:count], rest[count:]
    h_ref, qk_ref, v_ref, a_ref, lse_ref, *rest = rest
    wholes, sems = rest[:count], rest[count:]
    plan = Plan(pl.program_id(0), MICRO)
    if count:
        place = Place()
        moves = [
            Gather(place, layer, shards[i], wholes[i], sems[4 * i : 4 * i + 4])
            for i in range(count)
        ]
        plan.put(0, "start", place.greet, *[move.start for move in moves])
        if count == 1:
            plan.put(0, 6, moves[0].second)
            plan.put(1, 6, moves[0].third)
        else:
            one, two, three = moves
            plan.put(0, 4, one.second)
            plan.put(0, "end", two.second)
            plan.put(1, 2, one.third)
            plan.put(1, 3, three.second)
            plan.put(1, 7, two.third)
            plan.put(1, "end", three.third)
        plan.put(1, "end", *[move.finish for move in moves])
    plan.run("start")
    x = (x_ref[...].T if turned else x_ref[...]).astype(f32)
    rows = x.shape[0]
    h_ref[...] = x
    normed = (x * norm(x) * gain_ref[...]).astype(bf16)
    qk = nn(normed, weight_ref[:, :QK_WIDTH])
    v_ref[...] = nn(normed, weight_ref[:, QK_WIDTH + Q_WIDTH :]).astype(bf16)
    qk = rotate(qk, table_ref[:, :128], table_ref[:, 128:]).astype(bf16)
    qk_ref[:, :Q_WIDTH] = qk[:, :Q_WIDTH] * SCALE
    qk_ref[:, Q_WIDTH:] = qk[:, Q_WIDTH:]
    size = tile_of(rows)
    tiles = rows // size
    for tile in range(tiles):
        start = tile * size
        reach = start + size
        bias = mask_bias(column_ref, row_ref, start, size)
        outputs = []
        for group in range(KEY_VALUE_HEADS):
            lanes = slice(group * HEAD_WIDTH, (group + 1) * HEAD_WIDTH)
            klanes = slice(Q_WIDTH + group * HEAD_WIDTH, Q_WIDTH + (group + 1) * HEAD_WIDTH)
            queries = heads_stacked(qk_ref, start, size, group)
            scores = nt(qk_ref[:reach, klanes], queries) + bias
            peak = jnp.max(scores, axis=0, keepdims=True)
            expo = jnp.exp(scores - peak)
            total = jnp.sum(expo, axis=0, keepdims=True)
            mixed = tn(v_ref[:reach, lanes], expo.astype(bf16)) * (1.0 / total)
            outputs += heads_split(mixed, size)
            line = peak + jnp.log(total)
            for j in range(GROUP):
                lse_ref[group * GROUP + j : group * GROUP + j + 1, start:reach] = line[
                    :, j * size : (j + 1) * size
                ]
            plan.run(tile * KEY_VALUE_HEADS + group)
        a_ref[start:reach, :] = jnp.concatenate(outputs, axis=1).astype(bf16)
    out = nn(a_ref[...], weight_ref[:, QK_WIDTH : QK_WIDTH + Q_WIDTH])
    h_ref[...] = h_ref[...] + out * live_ref[...]
    for point in range(tiles * KEY_VALUE_HEADS, 9):
        plan.run(point)
    plan.run("end")


def attn_backward_kernel(
    count, turned, x_ref, dh_ref, column_ref, row_ref, live_ref, table_ref, gain_ref, weight_ref,
    qk_ref, v_ref, a_ref, lse_ref, *rest
):
    sources, rest = rest[:count], rest[count:]
    dx_ref, grad_ref, gain_grad_ref, *rest = rest
    results, rest = rest[:count], rest[count:]
    (n1t_ref, at_ref, c_ref, dqk_ref, dv_ref, da_ref, weight_line_ref, dqk_sum, dv_sum) = rest[:9]
    buffers = rest[9:]
    step = pl.program_id(0)
    plan = Plan(step, MICRO)
    if count:
        place = Place()
        moves = [
            Reduce(place, sources[i], results[i], buffers[11 * i : 11 * i + 11])
            for i in range(count)
        ]
        plan.put(0, "start", place.greet, *[move.start for move in moves])
        one, two = moves[:2]
        plan.put(0, 0, one.second, two.second)
        plan.put(0, 6, one.third)
        plan.put(1, 0, one.fourth)
        plan.put(1, 1, two.third)
        plan.put(1, 4, two.fourth)
        if count == 3:
            plan.put(0, 1, moves[2].second)
            plan.put(1, 8, moves[2].third)
            plan.put(1, "end", moves[2].fourth)
        plan.put(1, "end", *[move.finish for move in moves])
    plan.run("start")
    rows = dh_ref.shape[0]
    here = pl.ds(pl.multiple_of(step * rows, rows), rows)
    c = (dh_ref[...] * live_ref[...]).astype(bf16)
    c_ref[here, :] = c
    da = nt(c, weight_ref[:, QK_WIDTH : QK_WIDTH + Q_WIDTH]).astype(bf16)
    da_ref[...] = da
    a = a_ref[...]
    at_ref[:, here] = a.T
    product = da.astype(f32) * a.astype(f32)
    high = product.astype(bf16)
    low = (product - high.astype(f32)).astype(bf16)
    pick = (
        lax.broadcasted_iota(jnp.int32, (LSE_ROWS, Q_WIDTH), 1) // HEAD_WIDTH
        == lax.broadcasted_iota(jnp.int32, (LSE_ROWS, Q_WIDTH), 0)
    )
    pick = jnp.where(pick, 1.0, 0.0).astype(bf16)
    weight_line_ref[...] = nt(pick, high) + nt(pick, low)
    size = tile_of(rows)
    tiles = rows // size
    for tile in reversed(range(tiles)):
        start = tile * size
        reach = start + size
        bias = mask_bias(column_ref, row_ref, start, size)
        query_grads = []
        for group in range(KEY_VALUE_HEADS):
            lanes = slice(group * HEAD_WIDTH, (group + 1) * HEAD_WIDTH)
            klanes = slice(Q_WIDTH + group * HEAD_WIDTH, Q_WIDTH + (group + 1) * HEAD_WIDTH)
            queries = heads_stacked(qk_ref, start, size, group)
            upstream = heads_stacked(da_ref, start, size, group)
            keys = qk_ref[:reach, klanes]
            values = v_ref[:reach, lanes]
            probs = jnp.exp(nt(keys, queries) + bias - row_line(lse_ref, start, size, group))
            value_grad = nn(probs.astype(bf16), upstream)
            grad_probs = nt(values, upstream)
            grad_scores = (
                probs * (grad_probs - row_line(weight_line_ref, start, size, group))
            ).astype(bf16)
            key_grad = nn(grad_scores, queries)
            query_grads += heads_split(tn(keys, grad_scores) * SCALE, size)
            if reach == rows:
                dqk_sum[:, klanes] = key_grad
                dv_sum[:, lanes] = value_grad
            else:
                dqk_sum[:reach, klanes] += key_grad
                dv_sum[:reach, lanes] += value_grad
            plan.run((tiles - 1 - tile) * KEY_VALUE_HEADS + group)
        dqk_sum[start:reach, :Q_WIDTH] = jnp.concatenate(query_grads, axis=1)
    for point in range(tiles * KEY_VALUE_HEADS, 9):
        plan.run(point)
    dqk = rotate(dqk_sum[...], table_ref[:, :128], -table_ref[:, 128:]).astype(bf16)
    dqk_ref[here, :] = dqk
    dv = dv_sum[...].astype(bf16)
    dv_ref[here, :] = dv
    dn = nt(dqk, weight_ref[:, :QK_WIDTH]) + nt(dv, weight_ref[:, QK_WIDTH + Q_WIDTH :])
    x = (x_ref[...].T if turned else x_ref[...]).astype(f32)
    factor = norm(x)
    unit = x * factor
    gain = gain_ref[...]
    n1t_ref[:, here] = (unit * gain).astype(bf16).T
    scaled = dn * gain
    dx = dh_ref[...] + factor * (
        scaled - unit * jnp.mean(scaled * unit, axis=-1, keepdims=True)
    )
    dx_ref[...] = dx.T if turned else dx
    gain_part = jnp.sum(dn * unit, axis=0, keepdims=True)

    @pl.when(step == 0)
    def _():
        gain_grad_ref[...] = gain_part

    @pl.when(step > 0)
    def _():
        gain_grad_ref[...] += gain_part

    @pl.when(step == pl.num_programs(0) - 1)
    def _():
        grad_ref[:, :QK_WIDTH] = nn(n1t_ref[...], dqk_ref[...]).astype(bf16)
        grad_ref[:, QK_WIDTH : QK_WIDTH + Q_WIDTH] = nn(at_ref[...], c_ref[...]).astype(bf16)
        grad_ref[:, QK_WIDTH + Q_WIDTH :] = nn(n1t_ref[...], dv_ref[...]).astype(bf16)

    plan.run("end")


def ff_forward_kernel(
    layer, count, steps, h_ref, live_ref, gain_ref, wg_ref, wu_ref, wd_ref, *rest
):
    shards, (y_ref, *rest) = rest[:count], rest[count:]
    wholes, sems = rest[:count], rest[count:]
    plan = Plan(pl.program_id(0), steps)
    if count:
        place = Place()
        moves = [
            Gather(place, layer, shards[i], wholes[i], sems[4 * i : 4 * i + 4])
            for i in range(count)
        ]
        for move in moves:
            plan.put(steps * 2 // 6, "start", move.second)
            plan.put(steps * 5 // 6, "start", move.third)
            plan.put(steps - 1, "end", move.finish)
        plan.put(0, "start", place.greet, *[move.start for move in moves])
    plan.run("start")
    h = h_ref[...]
    normed = (h * norm(h) * gain_ref[...]).astype(bf16)
    gate = nn(normed, wg_ref[...])
    up = nn(normed, wu_ref[...])
    half = 0.5 * gate
    inner = ((half + half * jnp.tanh(half)) * up).astype(bf16)
    y_ref[...] = h + nn(inner, wd_ref[...]) * live_ref[...]
    plan.run("end")


def ff_backward_kernel(
    last, count, steps, h_ref, dy_ref, live_ref, gain_ref, wg_ref, wu_ref, wd_ref, *rest,
):
    sources, rest = rest[:count], rest[count:]
    if last:
        y_ref, *rest = rest
    dh_ref, gg_ref, gu_ref, gd_ref, gain_grad_ref, *rest = rest
    results, rest = rest[:count], rest[count:]
    n2t_ref, et_ref, m_ref, dg_ref, du_ref, *buffers = rest
    step = pl.program_id(0)
    plan = Plan(step, steps)
    if count:
        place = Place()
        moves = [
            Reduce(place, sources[i], results[i], buffers[11 * i : 11 * i + 11])
            for i in range(count)
        ]
        plan.put(0, "start", place.greet, *[move.start for move in moves])
        for move in moves:
            plan.put(steps * 1 // 6, "start", move.second)
            plan.put(steps * 4 // 6, "start", move.third)
            plan.put(steps * 5 // 6, "end", move.fourth)
            plan.put(steps - 1, "last", move.finish)
    plan.run("start")
    rows = h_ref.shape[0]
    here = pl.ds(pl.multiple_of(step * rows, rows), rows)
    h = h_ref[...]
    factor = norm(h)
    unit = h * factor
    gain = gain_ref[...]
    normed = (unit * gain).astype(bf16)
    n2t_ref[:, here] = normed.T
    live = live_ref[...]
    dy = (dy_ref[...].T if last else dy_ref[...]).astype(f32)
    e = (dy * live).astype(bf16)
    et_ref[:, here] = e.T
    gate = nn(normed, wg_ref[...])
    up = nn(normed, wu_ref[...])
    sig = 0.5 + 0.5 * jnp.tanh(0.5 * gate)
    silu = gate * sig
    inner = (silu * up).astype(bf16)
    m_ref[here, :] = inner
    dm = nt(e, wd_ref[...]).astype(bf16).astype(f32)
    dgate = (dm * up * (sig + silu * (1.0 - sig))).astype(bf16)
    dup = (dm * silu).astype(bf16)
    dg_ref[here, :] = dgate
    du_ref[here, :] = dup
    if last:
        y_ref[...] = (h + nn(inner, wd_ref[...]) * live).astype(bf16).T
    dn = nt(dgate, wg_ref[...]) + nt(dup, wu_ref[...])
    scaled = dn * gain
    dh_ref[...] = dy + factor * (scaled - unit * jnp.mean(scaled * unit, axis=-1, keepdims=True))
    gain_part = jnp.sum(dn * unit, axis=0, keepdims=True)

    plan.run("end")

    @pl.when(step == 0)
    def _():
        gain_grad_ref[...] = gain_part

    @pl.when(step > 0)
    def _():
        gain_grad_ref[...] += gain_part

    @pl.when(step == pl.num_programs(0) - 1)
    def _():
        ff = m_ref.shape[1]
        for first in range(0, ff, 512):
            cols = slice(first, first + 512)
            gg_ref[:, cols] = nn(n2t_ref[...], dg_ref[:, cols]).astype(bf16)
            gu_ref[:, cols] = nn(n2t_ref[...], du_ref[:, cols]).astype(bf16)
            gd_ref[cols, :] = nn(et_ref[...], m_ref[:, cols]).astype(bf16).T

    plan.run("last")


def row_spec(size, width):
    return pl.BlockSpec((size, width), lambda i: (i, 0))


def whole_spec(shape):
    return pl.BlockSpec(shape, lambda i: (0,) * len(shape), pipeline_mode=pl.Buffered(1))


def turned_spec(size, width):
    return pl.BlockSpec((width, size), lambda i: (0, i))


def still_spec(shape):
    return pl.BlockSpec(shape, lambda i: (0,) * len(shape))


def shape(dims, dtype):
    return jax.ShapeDtypeStruct(dims, dtype)


def params(collective_id=None, mib=62):
    extra = {}
    if collective_id is not None:
        extra = {"collective_id": collective_id, "has_side_effects": True}
    return pltpu.CompilerParams(
        vmem_limit_bytes=mib * 2**20, dimension_semantics=("arbitrary",), **extra
    )


def any_spec():
    return pl.BlockSpec(memory_space=pl.ANY)


def cost(flops, *arrays):
    return pl.CostEstimate(
        flops=int(flops),
        bytes_accessed=sum(int(a.size) * a.dtype.itemsize for a in arrays),
        transcendentals=0,
    )


def attn_forward(
    x, segment, live, table, gain, weight, turned, collective_id=None, layer=None, shards=()
):
    total, width = x.shape[::-1] if turned else x.shape
    copies, devices = lax.axis_size("rep"), lax.axis_size("fsdp")
    wholes = [shape((devices,) + w.shape[1:], bf16) for w in shards]
    sems = []
    for _ in shards:
        sems += Gather.semaphores(copies, devices // 2)
    size = total // MICRO
    outs = [
        shape((total, width), f32),
        shape((total, QK_WIDTH), bf16),
        shape((total, KV_WIDTH), bf16),
        shape((total, Q_WIDTH), bf16),
        shape((LSE_ROWS, total), f32),
    ]
    return pl.pallas_call(
        functools.partial(attn_forward_kernel, layer, len(shards), turned),
        grid=(MICRO,),
        in_specs=[
            turned_spec(size, width) if turned else row_spec(size, width),
            row_spec(size, 1),
            pl.BlockSpec((1, 1, size), lambda i: (i, 0, 0)),
            row_spec(size, 1),
            row_spec(size, 256),
            whole_spec(gain.shape),
            whole_spec(weight.shape),
        ]
        + [any_spec() for _ in shards],
        out_specs=[row_spec(size, o.shape[1]) for o in outs[:4]]
        + [pl.BlockSpec((LSE_ROWS, size), lambda i: (0, i))]
        + [any_spec() for _ in shards],
        out_shape=outs + wholes,
        scratch_shapes=sems,
        compiler_params=params(collective_id),
        cost_estimate=cost(2 * total * (width * 1536 + size * Q_WIDTH * 4), x, weight, *outs),
        name="attn_fwd",
    )(x, segment.reshape(-1, 1), segment.reshape(MICRO, 1, size), live, table, gain, weight, *shards)


def attn_backward(
    x, dh, segment, live, table, gain, weight, saved, turned, collective_id=None, sources=()
):
    total, width = dh.shape
    copies, devices = lax.axis_size("rep"), lax.axis_size("fsdp")
    sums = [shape(g.shape[1:], f32) for g in sources]
    buffers = []
    for g in sources:
        buffers += Reduce.scratch(g.shape[1:], copies, devices // 2)
    size = total // MICRO
    qk, v, a, lse = saved
    outs = [shape(x.shape, f32), shape(weight.shape, bf16), shape((1, width), f32)]
    x_spec = turned_spec(size, width) if turned else row_spec(size, width)
    return pl.pallas_call(
        functools.partial(attn_backward_kernel, len(sources), turned),
        grid=(MICRO,),
        in_specs=[
            x_spec,
            row_spec(size, width),
            row_spec(size, 1),
            pl.BlockSpec((1, 1, size), lambda i: (i, 0, 0)),
            row_spec(size, 1),
            row_spec(size, 256),
            whole_spec(gain.shape),
            whole_spec(weight.shape),
            row_spec(size, QK_WIDTH),
            row_spec(size, KV_WIDTH),
            row_spec(size, Q_WIDTH),
            pl.BlockSpec((LSE_ROWS, size), lambda i: (0, i)),
        ]
        + [any_spec() for _ in sources],
        out_specs=[x_spec, whole_spec(weight.shape), still_spec((1, width))]
        + [whole_spec(o.shape) for o in sums],
        out_shape=outs + sums,
        scratch_shapes=[
            pltpu.VMEM((width, total), bf16),
            pltpu.VMEM((Q_WIDTH, total), bf16),
            pltpu.VMEM((total, width), bf16),
            pltpu.VMEM((total, QK_WIDTH), bf16),
            pltpu.VMEM((total, KV_WIDTH), bf16),
            pltpu.VMEM((size, Q_WIDTH), bf16),
            pltpu.VMEM((LSE_ROWS, size), f32),
            pltpu.VMEM((size, QK_WIDTH), f32),
            pltpu.VMEM((size, KV_WIDTH), f32),
        ]
        + buffers,
        compiler_params=params(collective_id),
        cost_estimate=cost(2 * total * (width * 3072 + size * Q_WIDTH * 10), x, dh, weight, *outs),
        name="attn_bwd",
    )(
        x, dh, segment.reshape(-1, 1), segment.reshape(MICRO, 1, size), live, table, gain, weight,
        qk, v, a, lse, *sources,
    )


def reduce_kernel(count, *refs):
    sources, results, buffers = refs[:count], refs[count : 2 * count], refs[2 * count :]
    place = Place()
    moves = [
        Reduce(place, sources[i], results[i], buffers[11 * i : 11 * i + 11]) for i in range(count)
    ]
    place.greet()
    for stage in ("start", "second", "third", "fourth", "finish"):
        for move in moves:
            getattr(move, stage)()


def reduce_alone(collective_id, *sources):
    copies, devices = lax.axis_size("rep"), lax.axis_size("fsdp")
    buffers = []
    for g in sources:
        buffers += Reduce.scratch(g.shape[1:], copies, devices // 2)
    return pl.pallas_call(
        functools.partial(reduce_kernel, len(sources)),
        in_specs=[any_spec() for _ in sources],
        out_specs=[pl.BlockSpec(memory_space=pltpu.VMEM) for _ in sources],
        out_shape=[shape(g.shape[1:], f32) for g in sources],
        scratch_shapes=buffers,
        compiler_params=pltpu.CompilerParams(
            vmem_limit_bytes=32 * 2**20, collective_id=collective_id, has_side_effects=True
        ),
        name="reduce",
    )(*sources)


def ff_forward(h, live, gain, wg, wu, wd, collective_id=None, layer=None, shards=()):
    total, width = h.shape
    copies, devices = lax.axis_size("rep"), lax.axis_size("fsdp")
    wholes = [shape((devices,) + w.shape[1:], bf16) for w in shards]
    sems = []
    for _ in shards:
        sems += Gather.semaphores(copies, devices // 2)
    size = tile_of(total)
    out = shape((total, width), f32)
    return pl.pallas_call(
        functools.partial(ff_forward_kernel, layer, len(shards), total // size),
        grid=(total // size,),
        in_specs=[row_spec(size, width), row_spec(size, 1), whole_spec(gain.shape)]
        + [whole_spec(w.shape) for w in (wg, wu, wd)]
        + [any_spec() for _ in shards],
        out_specs=[row_spec(size, width)] + [any_spec() for _ in shards],
        out_shape=[out] + wholes,
        scratch_shapes=sems,
        compiler_params=params(collective_id),
        cost_estimate=cost(6 * total * wg.size, h, wg, wu, wd, out),
        name="ff_fwd",
    )(h, live, gain, wg, wu, wd, *shards)


def ff_backward(h, dy, live, gain, wg, wu, wd, last, collective_id=None, sources=()):
    total, width = h.shape
    ff = wg.shape[1]
    size = tile_of(total)
    outs = [
        shape((total, width), f32),
        shape(wg.shape, bf16),
        shape(wu.shape, bf16),
        shape(wd.shape, bf16),
        shape((1, width), f32),
    ]
    copies, devices = lax.axis_size("rep"), lax.axis_size("fsdp")
    sums = [shape(g.shape[1:], f32) for g in sources]
    buffers = []
    for g in sources:
        buffers += Reduce.scratch(g.shape[1:], copies, devices // 2)
    outs += sums
    specs = [row_spec(size, width)] + [whole_spec(o.shape) for o in outs[1:]]
    dy_spec = row_spec(size, width)
    if last:
        outs = [shape((width, total), bf16)] + outs
        dy_spec = turned_spec(size, width)
        specs = [dy_spec] + specs
    return pl.pallas_call(
        functools.partial(ff_backward_kernel, last, len(sources), total // size),
        grid=(total // size,),
        in_specs=[row_spec(size, width), dy_spec, row_spec(size, 1)]
        + [whole_spec(gain.shape)]
        + [whole_spec(w.shape) for w in (wg, wu, wd)]
        + [any_spec() for _ in sources],
        out_specs=specs,
        out_shape=outs,
        scratch_shapes=[
            pltpu.VMEM((width, total), bf16),
            pltpu.VMEM((width, total), bf16),
            pltpu.VMEM((total, ff), bf16),
            pltpu.VMEM((total, ff), bf16),
            pltpu.VMEM((total, ff), bf16),
        ]
        + buffers,
        compiler_params=params(collective_id),
        cost_estimate=cost(16 * total * wg.size, h, dy, wg, wu, wd, *outs),
        name="ff_bwd",
    )(h, dy, live, gain, wg, wu, wd, *sources)


def sum_shards(buffer):
    shard = lax.psum_scatter(buffer, "fsdp", scatter_dimension=0, tiled=False)
    return lax.psum(shard, "rep").astype(f32)


def local(
    tokens, segment, attn_gain, w_query, key_weight, value_weight, w_out, mlp_gain,
    gate_weight, up_weight, down_weight, cotangent,
):
    devices = lax.axis_size("fsdp")
    rows, ff = gate_weight.shape[1:]
    width = rows * devices
    down_rows = down_weight.shape[1]
    live, table = geometry(segment)

    gains = jnp.concatenate([attn_gain, mlp_gain]).reshape(1, 4 * rows)
    gains = jnp.pad(gains, ((0, 0), (0, QK_WIDTH + Q_WIDTH + KV_WIDTH - 4 * rows)))
    shards = (gate_weight, up_weight, down_weight)
    copies = lax.axis_size("rep")
    direct = all(can_cut(w.shape[1:], copies) for w in shards)
    attn_w = []
    for layer in range(DECODER_LAYERS):
        packed = jnp.concatenate(
            [w_query[layer], key_weight[layer], w_out[layer], value_weight[layer]], axis=1
        )
        if layer == 0:
            packed = jnp.concatenate([packed, gains])
            whole = lax.all_gather(packed, "fsdp", axis=0, tiled=False)
            all_gains = whole[:, rows, : 4 * rows].reshape(devices, 4, rows)
            all_gains = all_gains.transpose(1, 0, 2).reshape(4, 1, width).astype(f32)
            attn_w.append(whole[:, :rows].reshape(width, -1))
        else:
            attn_w.append(lax.all_gather(packed, "fsdp", axis=0, tiled=True))

    def whole(shard):
        gathered = lax.all_gather(shard, "fsdp", axis=0, tiled=False)
        return gathered

    def feed_of(gathered):
        gate, up, down = gathered
        return gate.reshape(width, ff), up.reshape(width, ff), down.reshape(ff, width)

    def split(grads):
        dims = ((rows, ff), (rows, ff), (down_rows, width))
        return [g.reshape((devices,) + d) for g, d in zip(grads, dims)]

    tokens, cotangent = tokens.T, cotangent.T
    args0 = (tokens, segment, live, table, all_gains[0], attn_w[0], True)
    if direct:
        down1 = whole(down_weight[1])
        h0, *kept0 = attn_forward(*args0, 0, 0, shards)
        kept0, feed0 = kept0[:4], feed_of(kept0[4:])
        x1, gate1 = ff_forward(h0, live, all_gains[2], *feed0, 1, 1, shards[:1])
    else:
        h0, *kept0 = attn_forward(*args0)
        feed0 = feed_of([whole(w[0]) for w in shards])
        x1 = ff_forward(h0, live, all_gains[2], *feed0)[0]
    args1 = (x1, segment, live, table, all_gains[1], attn_w[1], False)
    if direct:
        h1, *kept1 = attn_forward(*args1, 2, 1, shards[1:2])
        kept1, feed1 = kept1[:4], feed_of([gate1, kept1[4], down1])
    else:
        h1, *kept1 = attn_forward(*args1)
        feed1 = feed_of([whole(w[1]) for w in shards])
    out_tokens, dh1, gg1, gu1, gd1, mg1 = ff_backward(
        h1, cotangent, live, all_gains[3], *feed1, True
    )
    grads1 = split((gg1, gu1, gd1))
    args1 = (x1, dh1, segment, live, table, all_gains[1], attn_w[1], kept1, False)
    if direct:
        dx1, ga1, ag1, *sums1 = attn_backward(*args1, 3, grads1[:2])
    else:
        dx1, ga1, ag1 = attn_backward(*args1)
    ga1 = ga1.reshape(devices, rows, ff)
    args0 = (h0, dx1, live, all_gains[2], *feed0, False)
    if direct:
        dh0, gg0, gu0, gd0, mg0, down1, attn1 = ff_backward(*args0, 4, (grads1[2], ga1))
        sums1.append(down1)
    else:
        sums1, attn1 = [sum_shards(g) for g in grads1], sum_shards(ga1)
        dh0, gg0, gu0, gd0, mg0 = ff_backward(*args0)
    grads0 = split((gg0, gu0, gd0))
    args0 = (tokens, dh0, segment, live, table, all_gains[0], attn_w[0], kept0, True)
    if direct:
        dx0, ga0, ag0, *sums0 = attn_backward(*args0, 5, grads0)
    else:
        dx0, ga0, ag0 = attn_backward(*args0)
        sums0 = [sum_shards(g) for g in grads0]
    ga0 = ga0.reshape(devices, rows, ff)
    room = 512 * -(-4 * rows // 512)
    gain_grads = jnp.concatenate(
        [g.reshape(devices, 1, rows).astype(bf16) for g in (ag0, ag1, mg0, mg1)], axis=2
    )
    gain_grads = jnp.pad(gain_grads, ((0, 0), (0, 15), (0, room - 4 * rows)))
    if direct:
        attn0, last = reduce_alone(6, ga0, gain_grads)
    else:
        attn0, last = sum_shards(ga0), sum_shards(gain_grads)
    last = last[0]
    attn = jnp.stack([attn0, attn1])
    feed = [jnp.stack(pair) for pair in zip(sums0, sums1)]
    return (
        out_tokens.T,
        dx0.T,
        last[: 2 * rows].reshape(2, rows),
        attn[:, :, :Q_WIDTH],
        attn[:, :, Q_WIDTH:QK_WIDTH],
        attn[:, :, QK_WIDTH + Q_WIDTH :],
        attn[:, :, QK_WIDTH : QK_WIDTH + Q_WIDTH],
        last[2 * rows : 4 * rows].reshape(2, rows),
        *feed,
    )


def solution(mesh):
    rows = P(("rep", "fsdp"), None)
    flat, cube = P(None, "fsdp"), P(None, "fsdp", None)
    in_specs = (rows, P(("rep", "fsdp")), flat, cube, cube, cube, cube, flat, cube, cube, cube, rows)
    out_specs = (rows, rows, flat, cube, cube, cube, cube, flat, cube, cube, cube)
    return jax.shard_map(local, mesh=mesh, in_specs=in_specs, out_specs=out_specs, check_vma=False)
```

```python
import functools

import jax
import jax.numpy as jnp
from jax import lax
from jax.experimental import pallas as pl
from jax.experimental.pallas import tpu as pltpu
from jax.sharding import PartitionSpec as P

QUERY_HEADS = 9
KEY_VALUE_HEADS = 3
HEAD_WIDTH = 64
DECODER_LAYERS = 2
MICRO = 2
GROUP = QUERY_HEADS // KEY_VALUE_HEADS
Q_WIDTH = QUERY_HEADS * HEAD_WIDTH
KV_WIDTH = KEY_VALUE_HEADS * HEAD_WIDTH
QK_WIDTH = Q_WIDTH + KV_WIDTH
LSE_ROWS = 16
SCALE = HEAD_WIDTH ** (-0.5)

epsilon = 1e-05
rope_base = 100000.0
masked_fill = -1e30
f32 = jnp.float32
bf16 = jnp.bfloat16


def nn(left, right):
    return jnp.dot(left, right, preferred_element_type=f32)


def nt(left, right):
    return lax.dot_general(left, right, (((1,), (1,)), ((), ())), preferred_element_type=f32)


def tn(left, right):
    return lax.dot_general(left, right, (((0,), (0,)), ((), ())), preferred_element_type=f32)


def swap_halves(rows):
    lane = lax.broadcasted_iota(jnp.int32, rows.shape, 1)
    first = (lane % HEAD_WIDTH) < HEAD_WIDTH // 2
    return jnp.where(
        first, pltpu.roll(rows, 128 - HEAD_WIDTH // 2, 1), pltpu.roll(rows, HEAD_WIDTH // 2, 1)
    )


def rotate(rows, cosine, sine):
    parts = []
    for first in range(0, rows.shape[1], 128):
        slab = rows[:, first : first + 128]
        parts.append(slab * cosine + swap_halves(slab) * sine)
    return jnp.concatenate(parts, axis=1)


def tile_of(rows):
    return 256 if rows % 256 == 0 else rows


def heads_stacked(ref, start, size, group):
    first = group * GROUP * HEAD_WIDTH
    piece = ref[start : start + size, first : first + GROUP * HEAD_WIDTH]
    return jnp.concatenate(
        [piece[:, j * HEAD_WIDTH : (j + 1) * HEAD_WIDTH] for j in range(GROUP)], axis=0
    )


def heads_split(stacked, size):
    turned = stacked.T
    return [turned[j * size : (j + 1) * size] for j in range(GROUP)]


def mask_bias(column_ref, row_ref, start, size):
    reach = start + size
    shape = (reach, size)
    key = lax.broadcasted_iota(jnp.int32, shape, 0)
    query = lax.broadcasted_iota(jnp.int32, shape, 1) + start
    same = column_ref[:reach, :] == row_ref[0, :, start:reach]
    bias = jnp.where(same & (key <= query), 0.0, masked_fill)
    return jnp.concatenate([bias] * GROUP, axis=1)


def norm(rows):
    return lax.rsqrt(jnp.mean(rows * rows, axis=-1, keepdims=True) + epsilon)


def row_line(ref, start, size, group):
    return jnp.concatenate(
        [ref[group * GROUP + j : group * GROUP + j + 1, start : start + size] for j in range(GROUP)],
        axis=1,
    )


MESH_AXES = ("rep", "fsdp")


class Place:
    def __init__(self):
        self.copies = lax.axis_size("rep")
        self.line = lax.axis_size("fsdp") // 2
        self.r = lax.axis_index("rep")
        index = lax.axis_index("fsdp")
        self.z = index // 2
        self.c = index % 2

    def at(self, r, z, c):
        return (r, 2 * z + c)

    def partner(self):
        return self.at(self.r, self.z, 1 - self.c)

    def chip(self, k):
        return lax.rem(self.z + k, self.line)

    def replica(self, j):
        return lax.rem(self.r + j, self.copies)

    def greet(self):
        barrier = pltpu.get_barrier_semaphore()
        peers = [self.partner()]
        peers += [self.at(self.r, self.chip(k), self.c) for k in range(1, self.line)]
        peers += [self.at(self.replica(j), self.z, self.c) for j in range(1, self.copies)]
        for peer in peers:
            pl.semaphore_signal(barrier, inc=1, device_id=peer, device_id_type=pl.DeviceIdType.MESH)
        pl.semaphore_wait(barrier, len(peers))


def remote(source, target, send, receive, device):
    return pltpu.make_async_remote_copy(
        src_ref=source, dst_ref=target, send_sem=send, recv_sem=receive,
        device_id=device, device_id_type=pl.DeviceIdType.MESH,
    )


def part_of(dims, parts):
    rows, cols = dims
    if cols % (128 * parts) == 0:
        return 1, cols // parts
    return 0, rows // parts


def can_cut(dims, parts):
    rows, cols = dims
    return cols % (128 * parts) == 0 or rows % (16 * parts) == 0


def piece(ref, lead, dims, parts, index):
    axis, size = part_of(dims, parts)
    if axis == 1:
        return ref.at[lead, :, pl.ds(pl.multiple_of(index * size, 128), size)]
    return ref.at[lead, pl.ds(pl.multiple_of(index * size, 16), size), :]


def piece_dims(dims, parts):
    axis, size = part_of(dims, parts)
    return (dims[0], size) if axis == 1 else (size, dims[1])


class Gather:
    def __init__(self, place, shard, whole, sems):
        self.p, self.shard, self.whole, self.sems = place, shard, whole, sems
        self.dims = whole.shape[1:]
        self.parts = place.copies

    @staticmethod
    def semaphores(copies, line):
        return [
            pltpu.SemaphoreType.DMA((2, line)),
            pltpu.SemaphoreType.DMA((2, line, copies)),
            pltpu.SemaphoreType.DMA((2, line)),
            pltpu.SemaphoreType.DMA,
        ]

    def own(self):
        p = self.p
        return pltpu.make_async_copy(
            self.shard[0].at[self.shard[1]], self.whole.at[2 * p.z + p.c], self.sems[3]
        )

    def along(self, k):
        p = self.p
        return remote(
            piece(self.shard[0], self.shard[1], self.dims, self.parts, p.r),
            piece(self.whole, 2 * p.z + p.c, self.dims, self.parts, p.r),
            self.sems[0].at[0, k], self.sems[0].at[1, k], p.at(p.r, p.chip(k), p.c),
        )

    def across(self, k, j):
        p = self.p
        block = piece(self.whole, 2 * p.chip(p.line - k) + p.c, self.dims, self.parts, p.r)
        return remote(
            block, block, self.sems[1].at[0, k, j], self.sems[1].at[1, k, j],
            p.at(p.replica(j), p.z, p.c),
        )

    def pair(self, k):
        p = self.p
        block = self.whole.at[2 * p.chip(p.line - k) + p.c]
        return remote(block, block, self.sems[2].at[0, k], self.sems[2].at[1, k], p.partner())

    def others(self):
        return [(k, j) for k in range(1, self.p.line) for j in range(1, self.p.copies)]

    def line_start(self):
        for k in range(1, self.p.line):
            self.along(k).start()
        self.own().start()

    def line_end(self):
        for k in range(1, self.p.line):
            self.along(k).wait_recv()

    def across_start(self):
        for k, j in self.others():
            self.across(k, j).start()

    def across_end(self):
        for k, j in self.others():
            self.across(k, j).wait_recv()

    def pair_start(self):
        for k in range(self.p.line):
            self.pair(k).start()

    def line_done(self):
        self.own().wait()
        for k in range(1, self.p.line):
            self.along(k).wait_send()

    def across_done(self):
        for k, j in self.others():
            self.across(k, j).wait_send()

    def pair_done(self):
        for k in range(self.p.line):
            self.pair(k).wait()


def gathers(place, shards, wholes, sems):
    return [
        Gather(place, shards[i] if shards else None, wholes[i], sems[4 * i : 4 * i + 4])
        for i in range(len(wholes))
    ]


def gather_semaphores(count):
    copies, devices = lax.axis_size("rep"), lax.axis_size("fsdp")
    sems = []
    for _ in range(count):
        sems += Gather.semaphores(copies, devices // 2)
    return sems


class Reduce:
    def __init__(self, place, source, out, buffers, first=0, width=None):
        self.p, self.out, self.first = place, out, first
        self.source = source
        self.dims = (source.shape[1], width or source.shape[2])
        self.parts = place.copies
        (self.mine, self.theirs, self.across_in, self.line_out, self.line_in, self.final,
         self.s0, self.s1, self.s2, self.s3, self.s4) = buffers

    @staticmethod
    def scratch(dims, copies, line):
        small = piece_dims(dims, copies)
        return [
            pltpu.VMEM((line,) + tuple(dims), bf16),
            pltpu.VMEM((line,) + tuple(dims), bf16),
            pltpu.VMEM((copies, line) + small, bf16),
            pltpu.VMEM((line,) + small, bf16),
            pltpu.VMEM((line,) + small, bf16),
            pltpu.VMEM((copies,) + small, bf16),
            pltpu.SemaphoreType.DMA((2, line)),
            pltpu.SemaphoreType.DMA((line,)),
            pltpu.SemaphoreType.DMA((2, copies, line)),
            pltpu.SemaphoreType.DMA((2, line)),
            pltpu.SemaphoreType.DMA((2, copies)),
        ]

    def shard(self, index):
        if self.dims[1] == self.source.shape[2]:
            return self.source.at[index]
        return self.source.at[index, :, pl.ds(self.first, self.dims[1])]

    def pair(self, z):
        p = self.p
        return remote(
            self.shard(2 * z + 1 - p.c), self.theirs.at[z],
            self.s0.at[0, z], self.s0.at[1, z], p.partner(),
        )

    def load(self, z):
        return pltpu.make_async_copy(
            self.shard(2 * z + self.p.c), self.mine.at[z], self.s1.at[z]
        )

    def across(self, j, z):
        p = self.p
        return remote(
            piece(self.mine, z, self.dims, self.parts, p.replica(j)), self.across_in.at[j, z],
            self.s2.at[0, j, z], self.s2.at[1, j, z], p.at(p.replica(j), p.z, p.c),
        )

    def along(self, k):
        p = self.p
        return remote(
            self.line_out.at[p.chip(k)], self.line_in.at[k],
            self.s3.at[0, k], self.s3.at[1, k], p.at(p.r, p.chip(k), p.c),
        )

    def spread(self, j):
        p = self.p
        return remote(
            self.final.at[p.r], self.final.at[p.r],
            self.s4.at[0, j], self.s4.at[1, j], p.at(p.replica(j), p.z, p.c),
        )

    def start(self):
        for z in range(self.p.line):
            self.pair(z).start()
            self.load(z).start()

    def second(self):
        for z in range(self.p.line):
            self.load(z).wait()
            self.pair(z).wait_recv()
            self.mine[z] = (self.mine[z].astype(f32) + self.theirs[z].astype(f32)).astype(bf16)
            for j in range(1, self.p.copies):
                self.across(j, z).start()

    def third(self):
        for z in range(self.p.line):
            total = piece(self.mine, z, self.dims, self.parts, self.p.r)[...].astype(f32)
            for j in range(1, self.p.copies):
                self.across(j, z).wait_recv()
                total += self.across_in[j, z].astype(f32)
            self.line_out[z] = total.astype(bf16)
        for k in range(1, self.p.line):
            self.along(k).start()

    def fourth(self):
        total = self.line_out[self.p.z].astype(f32)
        for k in range(1, self.p.line):
            self.along(k).wait_recv()
            total += self.line_in[k].astype(f32)
        self.final[self.p.r] = total.astype(bf16)
        for j in range(1, self.p.copies):
            self.spread(j).start()

    def finish(self):
        self.write()
        for z in range(self.p.line):
            self.pair(z).wait_send()
            for j in range(1, self.p.copies):
                self.across(j, z).wait_send()
        for k in range(1, self.p.line):
            self.along(k).wait_send()

    def write(self):
        for j in range(1, self.p.copies):
            self.spread(j).wait()
        axis, size = part_of(self.dims, self.parts)
        for index in range(self.parts):
            here = index * size
            if axis == 1:
                here += self.first
                self.out[:, here : here + size] = self.final[index].astype(f32)
            else:
                self.out[here : here + size, :] = self.final[index].astype(f32)


class LineReduce(Reduce):
    @staticmethod
    def scratch(dims, copies, line):
        small = piece_dims(dims, copies)
        return [
            pltpu.VMEM((line,) + tuple(dims), bf16),
            pltpu.VMEM((line,) + tuple(dims), bf16),
            pltpu.VMEM((copies,) + small, bf16),
            pltpu.VMEM((1,) + tuple(dims), bf16),
            pltpu.VMEM((line,) + tuple(dims), bf16),
            pltpu.VMEM((copies,) + small, bf16),
            pltpu.SemaphoreType.DMA((2, line)),
            pltpu.SemaphoreType.DMA((line,)),
            pltpu.SemaphoreType.DMA((2, copies)),
            pltpu.SemaphoreType.DMA((2, line)),
            pltpu.SemaphoreType.DMA((2, copies)),
        ]

    def along(self, k):
        p = self.p
        return remote(
            self.mine.at[p.chip(k)], self.line_in.at[k],
            self.s3.at[0, k], self.s3.at[1, k], p.at(p.r, p.chip(k), p.c),
        )

    def across(self, j):
        p = self.p
        return remote(
            piece(self.line_out, 0, self.dims, self.parts, p.replica(j)), self.across_in.at[j],
            self.s2.at[0, j], self.s2.at[1, j], p.at(p.replica(j), p.z, p.c),
        )

    def second(self):
        for z in range(self.p.line):
            self.load(z).wait()
            self.pair(z).wait_recv()
            self.mine[z] = (self.mine[z].astype(f32) + self.theirs[z].astype(f32)).astype(bf16)
        for k in range(1, self.p.line):
            self.along(k).start()

    def third(self):
        total = self.mine[self.p.z].astype(f32)
        for k in range(1, self.p.line):
            self.along(k).wait_recv()
            total += self.line_in[k].astype(f32)
        self.line_out[0] = total.astype(bf16)
        for j in range(1, self.p.copies):
            self.across(j).start()

    def fourth(self):
        total = piece(self.line_out, 0, self.dims, self.parts, self.p.r)[...].astype(f32)
        for j in range(1, self.p.copies):
            self.across(j).wait_recv()
            total += self.across_in[j].astype(f32)
        self.final[self.p.r] = total.astype(bf16)
        for j in range(1, self.p.copies):
            self.spread(j).start()

    def finish(self):
        self.write()
        for z in range(self.p.line):
            self.pair(z).wait_send()
        for k in range(1, self.p.line):
            self.along(k).wait_send()
        for j in range(1, self.p.copies):
            self.across(j).wait_send()


def kinds_of(count):
    return [Reduce, Reduce, LineReduce][:count]


def reduce_buffers(sources):
    copies, devices = lax.axis_size("rep"), lax.axis_size("fsdp")
    buffers = []
    for kind, g in zip(kinds_of(len(sources)), sources):
        buffers += kind.scratch(g.shape[1:], copies, devices // 2)
    return buffers


def reduces(place, sources, results, buffers):
    return [
        kind(place, sources[i], results[i], buffers[11 * i : 11 * i + 11])
        for i, kind in enumerate(kinds_of(len(sources)))
    ]


class Plan:
    def __init__(self, step, steps):
        self.step, self.steps, self.at = step, steps, {}

    def put(self, when, point, *acts):
        self.at.setdefault((when, point), []).extend(acts)

    def run(self, point):
        for when in range(self.steps):
            acts = self.at.get((when, point), [])
            if acts:
                @pl.when(self.step == when)
                def _(acts=acts):
                    for act in acts:
                        act()


def feed_line(plan, points, moves):
    gate, up, down = moves
    (one, two), last = points[0], points[1]
    plan.put(one, two, gate.line_end, gate.across_start)
    plan.put(*last, up.line_end, down.line_end, gate.across_end, gate.across_done)
    plan.put(*last, *[move.line_done for move in moves])


def prepare_kernel(counts, column_ref, row_ref, frequency_ref, *refs):
    attn_count, feed_count = counts
    total = attn_count + feed_count
    shards, refs = refs[:total], refs[total:]
    live_ref, table_ref, *refs = refs
    wholes, sems = refs[:total], refs[total:]
    if total:
        place = Place()
        moves = gathers(place, [(ref, 0) for ref in shards], wholes, sems)
        first, feed = moves[:attn_count], moves[attn_count:]
        place.greet()
        for move in moves:
            move.line_start()
    size = row_ref.shape[2]
    live_ref[...] = jnp.where(column_ref[...] >= 0, 1.0, 0.0).astype(f32)
    key = lax.broadcasted_iota(jnp.int32, (size, size), 1)
    query = lax.broadcasted_iota(jnp.int32, (size, size), 0)
    positions = []
    for block in range(MICRO):
        same = column_ref[block * size : (block + 1) * size, :] == row_ref[block]
        earlier = jnp.where(same & (key < query), 1.0, 0.0)
        positions.append(jnp.sum(earlier, axis=1, keepdims=True))
    if total:
        for move in first:
            move.line_end()
            move.across_start()
    lane = lax.broadcasted_iota(jnp.int32, (size, 128), 1)
    sign = jnp.where(lane % HEAD_WIDTH < HEAD_WIDTH // 2, -1.0, 1.0)
    for block in range(MICRO):
        angles = positions[block] * frequency_ref[...]
        here = slice(block * size, (block + 1) * size)
        table_ref[here, :128] = jnp.cos(angles)
        table_ref[here, 128:] = jnp.sin(angles) * sign
    if total:
        gate = feed[0]
        gate.line_end()
        gate.across_start()
        for move in first:
            move.across_end()
            move.own().wait()
            move.pair_start()
        for move in feed[1:]:
            move.line_end()
        gate.across_end()
        gate.across_done()
        for move in feed:
            move.line_done()
        for move in first:
            for k in range(1, place.line):
                move.along(k).wait_send()
            move.across_done()
            move.pair_done()


def prepare(segment, shards=(), feed=(), collective_id=None):
    rows = segment.shape[0]
    size = rows // MICRO
    devices = lax.axis_size("fsdp")
    frequency = rope_base ** (-2.0 * jnp.arange(HEAD_WIDTH // 2, dtype=f32) / HEAD_WIDTH)
    frequency = jnp.concatenate([frequency] * 4)[None]
    everything = tuple(shards) + tuple(feed)
    wholes = [shape((devices,) + w.shape[1:], bf16) for w in everything]
    vmem = pl.BlockSpec(memory_space=pltpu.VMEM)
    extra = {}
    if everything:
        extra = {"collective_id": collective_id, "has_side_effects": True}
    return pl.pallas_call(
        functools.partial(prepare_kernel, (len(shards), len(feed))),
        in_specs=[vmem] * 3 + [any_spec() for _ in everything],
        out_specs=[vmem] * 2 + [any_spec() for _ in everything],
        out_shape=[shape((rows, 1), f32), shape((rows, 256), f32)] + wholes,
        scratch_shapes=gather_semaphores(len(everything)),
        compiler_params=pltpu.CompilerParams(vmem_limit_bytes=62 * 2**20, **extra),
        name="prepare",
    )(segment.reshape(-1, 1), segment.reshape(MICRO, 1, size), frequency, *everything)


def attn_forward_kernel(
    row, count, turned, x_ref, column_ref, row_ref, live_ref, table_ref, gain_ref, weight_ref,
    *rest
):
    h_ref, qk_ref, v_ref, a_ref, lse_ref, *rest = rest[count:]
    wholes, sems = rest[:count], rest[count:]
    plan = Plan(pl.program_id(0), MICRO)
    if count:
        place = Place()
        gate, up, down = gathers(place, (), wholes, sems)
        plan.put(0, "start", place.greet, up.across_start, down.across_start, gate.pair_start)
        plan.put(0, "end", up.across_end, up.pair_start)
        plan.put(1, 6, down.across_end, down.pair_start)
        plan.put(1, "end", gate.pair_done, up.across_done, up.pair_done)
        plan.put(1, "end", down.across_done, down.pair_done)
    plan.run("start")
    x = (x_ref[...].T if turned else x_ref[...]).astype(f32)
    rows = x.shape[0]
    h_ref[...] = x
    normed = (x * norm(x) * gain_ref[row : row + 1, :]).astype(bf16)
    qk = nn(normed, weight_ref[:, :QK_WIDTH])
    v_ref[...] = nn(normed, weight_ref[:, QK_WIDTH + Q_WIDTH :]).astype(bf16)
    qk = rotate(qk, table_ref[:, :128], table_ref[:, 128:]).astype(bf16)
    qk_ref[:, :Q_WIDTH] = qk[:, :Q_WIDTH] * SCALE
    qk_ref[:, Q_WIDTH:] = qk[:, Q_WIDTH:]
    size = tile_of(rows)
    tiles = rows // size
    for tile in range(tiles):
        start = tile * size
        reach = start + size
        bias = mask_bias(column_ref, row_ref, start, size)
        outputs = []
        for group in range(KEY_VALUE_HEADS):
            lanes = slice(group * HEAD_WIDTH, (group + 1) * HEAD_WIDTH)
            klanes = slice(Q_WIDTH + group * HEAD_WIDTH, Q_WIDTH + (group + 1) * HEAD_WIDTH)
            queries = heads_stacked(qk_ref, start, size, group)
            scores = nt(qk_ref[:reach, klanes], queries) + bias
            peak = jnp.max(scores, axis=0, keepdims=True)
            expo = jnp.exp(scores - peak)
            total = jnp.sum(expo, axis=0, keepdims=True)
            mixed = tn(v_ref[:reach, lanes], expo.astype(bf16)) * (1.0 / total)
            outputs += heads_split(mixed, size)
            line = peak + jnp.log(total)
            for j in range(GROUP):
                lse_ref[group * GROUP + j : group * GROUP + j + 1, start:reach] = line[
                    :, j * size : (j + 1) * size
                ]
            plan.run(tile * KEY_VALUE_HEADS + group)
        a_ref[start:reach, :] = jnp.concatenate(outputs, axis=1).astype(bf16)
    out = nn(a_ref[...], weight_ref[:, QK_WIDTH : QK_WIDTH + Q_WIDTH])
    h_ref[...] = h_ref[...] + out * live_ref[...]
    for point in range(tiles * KEY_VALUE_HEADS, 9):
        plan.run(point)
    plan.run("end")


def attn_backward_kernel(
    row, count, turned, x_ref, dh_ref, column_ref, row_ref, live_ref, table_ref, gain_ref, weight_ref,
    qk_ref, v_ref, a_ref, lse_ref, *rest
):
    sources, rest = rest[:count], rest[count:]
    dx_ref, grad_ref, gain_grad_ref, *rest = rest
    results, rest = rest[:count], rest[count:]
    (n1t_ref, at_ref, c_ref, dqk_ref, dv_ref, da_ref, weight_line_ref, dqk_sum, dv_sum) = rest[:9]
    buffers = rest[9:]
    step = pl.program_id(0)
    plan = Plan(step, MICRO)
    if count:
        place = Place()
        moves = reduces(place, sources, results, buffers)
        plan.put(0, "start", place.greet, *[move.start for move in moves])
        one, two = moves[:2]
        plan.put(0, 0, one.second, two.second)
        plan.put(0, 8, one.third)
        plan.put(1, 2, two.third)
        if count == 3:
            plan.put(0, 0, moves[2].second)
            plan.put(1, 3, moves[2].third, one.fourth)
            plan.put(1, 6, moves[2].fourth)
        else:
            plan.put(1, 1, one.fourth)
        plan.put(1, "grads", two.fourth)
        plan.put(1, "end", *[move.finish for move in moves])
    plan.run("start")
    rows = dh_ref.shape[0]
    here = pl.ds(pl.multiple_of(step * rows, rows), rows)
    c = (dh_ref[...] * live_ref[...]).astype(bf16)
    c_ref[here, :] = c
    da = nt(c, weight_ref[:, QK_WIDTH : QK_WIDTH + Q_WIDTH]).astype(bf16)
    da_ref[...] = da
    a = a_ref[...]
    at_ref[:, here] = a.T
    product = da.astype(f32) * a.astype(f32)
    high = product.astype(bf16)
    low = (product - high.astype(f32)).astype(bf16)
    pick = (
        lax.broadcasted_iota(jnp.int32, (LSE_ROWS, Q_WIDTH), 1) // HEAD_WIDTH
        == lax.broadcasted_iota(jnp.int32, (LSE_ROWS, Q_WIDTH), 0)
    )
    pick = jnp.where(pick, 1.0, 0.0).astype(bf16)
    weight_line_ref[...] = nt(pick, high) + nt(pick, low)
    size = tile_of(rows)
    tiles = rows // size
    for tile in reversed(range(tiles)):
        start = tile * size
        reach = start + size
        bias = mask_bias(column_ref, row_ref, start, size)
        query_grads = []
        for group in range(KEY_VALUE_HEADS):
            lanes = slice(group * HEAD_WIDTH, (group + 1) * HEAD_WIDTH)
            klanes = slice(Q_WIDTH + group * HEAD_WIDTH, Q_WIDTH + (group + 1) * HEAD_WIDTH)
            queries = heads_stacked(qk_ref, start, size, group)
            upstream = heads_stacked(da_ref, start, size, group)
            keys = qk_ref[:reach, klanes]
            values = v_ref[:reach, lanes]
            probs = jnp.exp(nt(keys, queries) + bias - row_line(lse_ref, start, size, group))
            value_grad = nn(probs.astype(bf16), upstream)
            grad_probs = nt(values, upstream)
            grad_scores = (
                probs * (grad_probs - row_line(weight_line_ref, start, size, group))
            ).astype(bf16)
            key_grad = nn(grad_scores, queries)
            query_grads += heads_split(tn(keys, grad_scores) * SCALE, size)
            if reach == rows:
                dqk_sum[:, klanes] = key_grad
                dv_sum[:, lanes] = value_grad
            else:
                dqk_sum[:reach, klanes] += key_grad
                dv_sum[:reach, lanes] += value_grad
            plan.run((tiles - 1 - tile) * KEY_VALUE_HEADS + group)
        dqk_sum[start:reach, :Q_WIDTH] = jnp.concatenate(query_grads, axis=1)
    for point in range(tiles * KEY_VALUE_HEADS, 9):
        plan.run(point)
    dqk = rotate(dqk_sum[...], table_ref[:, :128], -table_ref[:, 128:]).astype(bf16)
    dqk_ref[here, :] = dqk
    dv = dv_sum[...].astype(bf16)
    dv_ref[here, :] = dv
    dn = nt(dqk, weight_ref[:, :QK_WIDTH]) + nt(dv, weight_ref[:, QK_WIDTH + Q_WIDTH :])
    x = (x_ref[...].T if turned else x_ref[...]).astype(f32)
    factor = norm(x)
    unit = x * factor
    gain = gain_ref[row : row + 1, :]
    n1t_ref[:, here] = (unit * gain).astype(bf16).T
    scaled = dn * gain
    dx = dh_ref[...] + factor * (
        scaled - unit * jnp.mean(scaled * unit, axis=-1, keepdims=True)
    )
    dx_ref[...] = dx.T if turned else dx
    gain_part = jnp.sum(dn * unit, axis=0, keepdims=True)

    @pl.when(step == 0)
    def _():
        gain_grad_ref[...] = gain_part

    @pl.when(step > 0)
    def _():
        gain_grad_ref[...] += gain_part

    plan.run("grads")

    @pl.when(step == pl.num_programs(0) - 1)
    def _():
        grad_ref[:, :QK_WIDTH] = nn(n1t_ref[...], dqk_ref[...]).astype(bf16)
        grad_ref[:, QK_WIDTH : QK_WIDTH + Q_WIDTH] = nn(at_ref[...], c_ref[...]).astype(bf16)
        grad_ref[:, QK_WIDTH + Q_WIDTH :] = nn(n1t_ref[...], dv_ref[...]).astype(bf16)

    plan.run("end")


def ff_forward_kernel(
    row, layer, count, steps, h_ref, live_ref, gain_ref, wg_ref, wu_ref, wd_ref, *rest
):
    shards, (y_ref, *rest) = rest[:count], rest[count:]
    wholes, sems = rest[:count], rest[count:]
    plan = Plan(pl.program_id(0), steps)
    if count:
        place = Place()
        moves = gathers(place, [(ref, layer) for ref in shards], wholes, sems)
        plan.put(0, "start", place.greet, *[move.line_start for move in moves])
        feed_line(plan, ((steps * 2 // 6, "end"), (steps - 1, "end")), moves)
    plan.run("start")
    h = h_ref[...]
    normed = (h * norm(h) * gain_ref[row : row + 1, :]).astype(bf16)
    gate = nn(normed, wg_ref[...])
    up = nn(normed, wu_ref[...])
    half = 0.5 * gate
    inner = ((half + half * jnp.tanh(half)) * up).astype(bf16)
    y_ref[...] = h + nn(inner, wd_ref[...]) * live_ref[...]
    plan.run("end")


def ff_backward_kernel(
    row, last, count, steps, h_ref, dy_ref, live_ref, gain_ref, wg_ref, wu_ref, wd_ref, *rest,
):
    sources, rest = rest[:count], rest[count:]
    if last:
        y_ref, *rest = rest
    dh_ref, gg_ref, gu_ref, gd_ref, gain_grad_ref, *rest = rest
    results, rest = rest[:count], rest[count:]
    n2t_ref, et_ref, m_ref, dg_ref, du_ref, *buffers = rest
    step = pl.program_id(0)
    plan = Plan(step, steps)
    if count:
        place = Place()
        one, two = reduces(place, sources, results, buffers)
        plan.put(0, "start", place.greet, one.start, two.start)
        plan.put(0, "middle", one.second, two.second)
        plan.put(steps * 3 // 6, "middle", one.third)
        plan.put(steps * 4 // 6, "end", one.fourth, two.third)
        plan.put(steps - 1, "half", two.fourth)
        plan.put(steps - 1, "last", one.finish, two.finish)
    plan.run("start")
    rows = h_ref.shape[0]
    here = pl.ds(pl.multiple_of(step * rows, rows), rows)
    h = h_ref[...]
    factor = norm(h)
    unit = h * factor
    gain = gain_ref[row : row + 1, :]
    normed = (unit * gain).astype(bf16)
    n2t_ref[:, here] = normed.T
    live = live_ref[...]
    dy = (dy_ref[...].T if last else dy_ref[...]).astype(f32)
    e = (dy * live).astype(bf16)
    et_ref[:, here] = e.T
    gate = nn(normed, wg_ref[...])
    up = nn(normed, wu_ref[...])
    sig = 0.5 + 0.5 * jnp.tanh(0.5 * gate)
    silu = gate * sig
    inner = (silu * up).astype(bf16)
    m_ref[here, :] = inner
    plan.run("middle")
    dm = nt(e, wd_ref[...]).astype(bf16).astype(f32)
    dgate = (dm * up * (sig + silu * (1.0 - sig))).astype(bf16)
    dup = (dm * silu).astype(bf16)
    dg_ref[here, :] = dgate
    du_ref[here, :] = dup
    if last:
        y_ref[...] = (h + nn(inner, wd_ref[...]) * live).astype(bf16).T
    dn = nt(dgate, wg_ref[...]) + nt(dup, wu_ref[...])
    scaled = dn * gain
    dh_ref[...] = dy + factor * (scaled - unit * jnp.mean(scaled * unit, axis=-1, keepdims=True))
    gain_part = jnp.sum(dn * unit, axis=0, keepdims=True)

    plan.run("end")

    @pl.when(step == 0)
    def _():
        gain_grad_ref[...] = gain_part

    @pl.when(step > 0)
    def _():
        gain_grad_ref[...] += gain_part

    def weight_grads(first):
        cols = slice(first, first + 512)
        gg_ref[:, cols] = nn(n2t_ref[...], dg_ref[:, cols]).astype(bf16)
        gu_ref[:, cols] = nn(n2t_ref[...], du_ref[:, cols]).astype(bf16)
        gd_ref[cols, :] = nn(et_ref[...], m_ref[:, cols]).astype(bf16).T

    ff = m_ref.shape[1]

    @pl.when(step == steps - 1)
    def _():
        weight_grads(0)

    plan.run("half")

    @pl.when(step == steps - 1)
    def _():
        for first in range(512, ff, 512):
            weight_grads(first)

    plan.run("last")


def row_spec(size, width):
    return pl.BlockSpec((size, width), lambda i: (i, 0))


def whole_spec(shape):
    return pl.BlockSpec(shape, lambda i: (0,) * len(shape), pipeline_mode=pl.Buffered(1))


def turned_spec(size, width):
    return pl.BlockSpec((width, size), lambda i: (0, i))


def still_spec(shape):
    return pl.BlockSpec(shape, lambda i: (0,) * len(shape))


def shape(dims, dtype):
    return jax.ShapeDtypeStruct(dims, dtype)


def params(collective_id=None, mib=62):
    extra = {}
    if collective_id is not None:
        extra = {"collective_id": collective_id, "has_side_effects": True}
    return pltpu.CompilerParams(
        vmem_limit_bytes=mib * 2**20, dimension_semantics=("arbitrary",), **extra
    )


def any_spec():
    return pl.BlockSpec(memory_space=pl.ANY)


def cost(flops, *arrays):
    return pl.CostEstimate(
        flops=int(flops),
        bytes_accessed=sum(int(a.size) * a.dtype.itemsize for a in arrays),
        transcendentals=0,
    )


def attn_forward(
    x, segment, live, table, gain, weight, row, turned, collective_id=None, halves=()
):
    total, width = x.shape[::-1] if turned else x.shape
    size = total // MICRO
    outs = [
        shape((total, width), f32),
        shape((total, QK_WIDTH), bf16),
        shape((total, KV_WIDTH), bf16),
        shape((total, Q_WIDTH), bf16),
        shape((LSE_ROWS, total), f32),
    ]
    return pl.pallas_call(
        functools.partial(attn_forward_kernel, row, len(halves), turned),
        grid=(MICRO,),
        in_specs=[
            turned_spec(size, width) if turned else row_spec(size, width),
            row_spec(size, 1),
            pl.BlockSpec((1, 1, size), lambda i: (i, 0, 0)),
            row_spec(size, 1),
            row_spec(size, 256),
            whole_spec(gain.shape),
            whole_spec(weight.shape),
        ]
        + [any_spec() for _ in halves],
        out_specs=[row_spec(size, o.shape[1]) for o in outs[:4]]
        + [pl.BlockSpec((LSE_ROWS, size), lambda i: (0, i))]
        + [any_spec() for _ in halves],
        out_shape=outs + [shape(w.shape, bf16) for w in halves],
        scratch_shapes=gather_semaphores(len(halves)),
        input_output_aliases={7 + k: 5 + k for k in range(len(halves))},
        compiler_params=params(collective_id),
        cost_estimate=cost(2 * total * (width * 1536 + size * Q_WIDTH * 4), x, weight, *outs),
        name="attn_fwd",
    )(x, segment.reshape(-1, 1), segment.reshape(MICRO, 1, size), live, table, gain, weight, *halves)


def attn_backward(
    x, dh, segment, live, table, gain, weight, saved, row, turned, collective_id=None, sources=()
):
    total, width = dh.shape
    sums = [shape(g.shape[1:], f32) for g in sources]
    buffers = reduce_buffers(sources)
    size = total // MICRO
    qk, v, a, lse = saved
    outs = [shape(x.shape, f32), shape(weight.shape, bf16), shape((1, width), f32)]
    x_spec = turned_spec(size, width) if turned else row_spec(size, width)
    return pl.pallas_call(
        functools.partial(attn_backward_kernel, row, len(sources), turned),
        grid=(MICRO,),
        in_specs=[
            x_spec,
            row_spec(size, width),
            row_spec(size, 1),
            pl.BlockSpec((1, 1, size), lambda i: (i, 0, 0)),
            row_spec(size, 1),
            row_spec(size, 256),
            whole_spec(gain.shape),
            whole_spec(weight.shape),
            row_spec(size, QK_WIDTH),
            row_spec(size, KV_WIDTH),
            row_spec(size, Q_WIDTH),
            pl.BlockSpec((LSE_ROWS, size), lambda i: (0, i)),
        ]
        + [any_spec() for _ in sources],
        out_specs=[x_spec, whole_spec(weight.shape), still_spec((1, width))]
        + [whole_spec(o.shape) for o in sums],
        out_shape=outs + sums,
        scratch_shapes=[
            pltpu.VMEM((width, total), bf16),
            pltpu.VMEM((Q_WIDTH, total), bf16),
            pltpu.VMEM((total, width), bf16),
            pltpu.VMEM((total, QK_WIDTH), bf16),
            pltpu.VMEM((total, KV_WIDTH), bf16),
            pltpu.VMEM((size, Q_WIDTH), bf16),
            pltpu.VMEM((LSE_ROWS, size), f32),
            pltpu.VMEM((size, QK_WIDTH), f32),
            pltpu.VMEM((size, KV_WIDTH), f32),
        ]
        + buffers,
        compiler_params=params(collective_id),
        cost_estimate=cost(2 * total * (width * 3072 + size * Q_WIDTH * 10), x, dh, weight, *outs),
        name="attn_bwd",
    )(
        x, dh, segment.reshape(-1, 1), segment.reshape(MICRO, 1, size), live, table, gain, weight,
        qk, v, a, lse, *sources,
    )


CHUNK = 512


def windows(sources):
    return [(i, first) for i, g in enumerate(sources) for first in range(0, g.shape[2], CHUNK)]


def reduce_kernel(count, *refs):
    sources, results, buffers = refs[:count], refs[count : 2 * count], refs[2 * count :]
    place = Place()
    moves = [
        Reduce(place, sources[i], results[i], buffers[11 * n : 11 * n + 11], first, CHUNK)
        for n, (i, first) in enumerate(windows(sources))
    ]
    place.greet()
    for stage in ("start", "second", "third", "fourth", "finish"):
        for move in moves:
            getattr(move, stage)()


def reduce_alone(collective_id, *sources):
    copies, devices = lax.axis_size("rep"), lax.axis_size("fsdp")
    buffers = []
    for i, _ in windows(sources):
        buffers += Reduce.scratch((sources[i].shape[1], CHUNK), copies, devices // 2)
    return pl.pallas_call(
        functools.partial(reduce_kernel, len(sources)),
        in_specs=[any_spec() for _ in sources],
        out_specs=[pl.BlockSpec(memory_space=pltpu.VMEM) for _ in sources],
        out_shape=[shape(g.shape[1:], f32) for g in sources],
        scratch_shapes=buffers,
        compiler_params=pltpu.CompilerParams(
            vmem_limit_bytes=32 * 2**20, collective_id=collective_id, has_side_effects=True
        ),
        name="reduce",
    )(*sources)


def ff_forward(h, live, gain, wg, wu, wd, row, collective_id=None, layer=None, shards=()):
    total, width = h.shape
    devices = lax.axis_size("fsdp")
    wholes = [shape((devices,) + w.shape[1:], bf16) for w in shards]
    size = tile_of(total)
    out = shape((total, width), f32)
    return pl.pallas_call(
        functools.partial(ff_forward_kernel, row, layer, len(shards), total // size),
        grid=(total // size,),
        in_specs=[row_spec(size, width), row_spec(size, 1), whole_spec(gain.shape)]
        + [whole_spec(w.shape) for w in (wg, wu, wd)]
        + [any_spec() for _ in shards],
        out_specs=[row_spec(size, width)] + [any_spec() for _ in shards],
        out_shape=[out] + wholes,
        scratch_shapes=gather_semaphores(len(shards)),
        compiler_params=params(collective_id),
        cost_estimate=cost(6 * total * wg.size, h, wg, wu, wd, out),
        name="ff_fwd",
    )(h, live, gain, wg, wu, wd, *shards)


def ff_backward(h, dy, live, gain, wg, wu, wd, row, last, collective_id=None, sources=()):
    total, width = h.shape
    ff = wg.shape[1]
    size = tile_of(total)
    outs = [
        shape((total, width), f32),
        shape(wg.shape, bf16),
        shape(wu.shape, bf16),
        shape(wd.shape, bf16),
        shape((1, width), f32),
    ]
    sums = [shape(g.shape[1:], f32) for g in sources]
    buffers = reduce_buffers(sources)
    outs += sums
    specs = [row_spec(size, width)] + [whole_spec(o.shape) for o in outs[1:]]
    dy_spec = row_spec(size, width)
    if last:
        outs = [shape((width, total), bf16)] + outs
        dy_spec = turned_spec(size, width)
        specs = [dy_spec] + specs
    return pl.pallas_call(
        functools.partial(ff_backward_kernel, row, last, len(sources), total // size),
        grid=(total // size,),
        in_specs=[row_spec(size, width), dy_spec, row_spec(size, 1)]
        + [whole_spec(gain.shape)]
        + [whole_spec(w.shape) for w in (wg, wu, wd)]
        + [any_spec() for _ in sources],
        out_specs=specs,
        out_shape=outs,
        scratch_shapes=[
            pltpu.VMEM((width, total), bf16),
            pltpu.VMEM((width, total), bf16),
            pltpu.VMEM((total, ff), bf16),
            pltpu.VMEM((total, ff), bf16),
            pltpu.VMEM((total, ff), bf16),
        ]
        + buffers,
        compiler_params=params(collective_id),
        cost_estimate=cost(16 * total * wg.size, h, dy, wg, wu, wd, *outs),
        name="ff_bwd",
    )(h, dy, live, gain, wg, wu, wd, *sources)


def sum_shards(buffer):
    shard = lax.psum_scatter(buffer, "fsdp", scatter_dimension=0, tiled=False)
    return lax.psum(shard, "rep").astype(f32)


def local(
    tokens, segment, attn_gain, w_query, key_weight, value_weight, w_out, mlp_gain,
    gate_weight, up_weight, down_weight, cotangent,
):
    devices = lax.axis_size("fsdp")
    rows, ff = gate_weight.shape[1:]
    width = rows * devices
    down_rows = down_weight.shape[1]
    copies = lax.axis_size("rep")
    shards = (gate_weight, up_weight, down_weight)
    packed_gains = jnp.concatenate([attn_gain, mlp_gain]).reshape(1, 4 * rows)
    room = CHUNK * -(-4 * rows // CHUNK)
    packed_gains = jnp.pad(packed_gains, ((0, 15), (0, room - 4 * rows)))[None]
    packed = [
        jnp.concatenate([w_query[i], key_weight[i], w_out[i], value_weight[i]], axis=1)[None]
        for i in range(DECODER_LAYERS)
    ]
    direct = all(can_cut(w.shape[1:], copies) for w in shards) and can_cut((16, CHUNK), copies)

    def whole(shard):
        return lax.all_gather(shard, "fsdp", axis=0, tiled=True)

    def feed_of(gathered):
        gate, up, down = gathered
        return gate.reshape(width, ff), up.reshape(width, ff), down.reshape(ff, width)

    def split(grads):
        dims = ((rows, ff), (rows, ff), (down_rows, width))
        return [g.reshape((devices,) + d) for g, d in zip(grads, dims)]

    tokens, cotangent = tokens.T, cotangent.T
    if direct:
        live, table, weight0, gains, *feed0 = prepare(
            segment, (packed[0], packed_gains), shards, 0
        )
        packed[1], live = lax.optimization_barrier((packed[1], live))
    else:
        live, table = prepare(segment)
        weight0, gains = whole(packed[0]), whole(packed_gains)
    attn_w = [weight0.reshape(width, ff), whole(packed[1]).reshape(width, ff)]
    gains = gains[:, 0, : 4 * rows].reshape(devices, 4, rows)
    gains = gains.transpose(1, 0, 2).reshape(4, width).astype(f32)
    args0 = (tokens, segment, live, table, gains, attn_w[0], 0, True)
    if direct:
        h0, *kept0 = attn_forward(*args0, 1, feed0)
        kept0, feed0 = kept0[:4], feed_of(kept0[4:])
        x1, *feed1 = ff_forward(h0, live, gains, *feed0, 2, 2, 1, shards)
    else:
        h0, *kept0 = attn_forward(*args0)
        feed0 = feed_of([whole(w[0]) for w in shards])
        x1 = ff_forward(h0, live, gains, *feed0, 2)[0]
    args1 = (x1, segment, live, table, gains, attn_w[1], 1, False)
    if direct:
        h1, *kept1 = attn_forward(*args1, 3, feed1)
        kept1, feed1 = kept1[:4], feed_of(kept1[4:])
    else:
        h1, *kept1 = attn_forward(*args1)
        feed1 = feed_of([whole(w[1]) for w in shards])
    out_tokens, dh1, gg1, gu1, gd1, mg1 = ff_backward(
        h1, cotangent, live, gains, *feed1, 3, True
    )
    grads1 = split((gg1, gu1, gd1))
    args1 = (x1, dh1, segment, live, table, gains, attn_w[1], kept1, 1, False)
    if direct:
        dx1, ga1, ag1, *sums1 = attn_backward(*args1, 4, grads1[:2])
    else:
        dx1, ga1, ag1 = attn_backward(*args1)
    ga1 = ga1.reshape(devices, rows, ff)
    args0 = (h0, dx1, live, gains, *feed0, 2, False)
    if direct:
        dh0, gg0, gu0, gd0, mg0, down1, attn1 = ff_backward(*args0, 5, (grads1[2], ga1))
        sums1.append(down1)
    else:
        sums1, attn1 = [sum_shards(g) for g in grads1], sum_shards(ga1)
        dh0, gg0, gu0, gd0, mg0 = ff_backward(*args0)
    grads0 = split((gg0, gu0, gd0))
    args0 = (tokens, dh0, segment, live, table, gains, attn_w[0], kept0, 0, True)
    if direct:
        dx0, ga0, ag0, *sums0 = attn_backward(*args0, 6, grads0)
    else:
        dx0, ga0, ag0 = attn_backward(*args0)
        sums0 = [sum_shards(g) for g in grads0]
    ga0 = ga0.reshape(devices, rows, ff)
    gain_grads = jnp.concatenate(
        [g.reshape(devices, 1, rows).astype(bf16) for g in (ag0, ag1, mg0, mg1)], axis=2
    )
    gain_grads = jnp.pad(gain_grads, ((0, 0), (0, 15), (0, room - 4 * rows)))
    if direct:
        attn0, last = reduce_alone(7, ga0, gain_grads)
    else:
        attn0, last = sum_shards(ga0), sum_shards(gain_grads)
    last = last[0]
    attn = jnp.stack([attn0, attn1])
    feed = [jnp.stack(pair) for pair in zip(sums0, sums1)]
    return (
        out_tokens.T,
        dx0.T,
        last[: 2 * rows].reshape(2, rows),
        attn[:, :, :Q_WIDTH],
        attn[:, :, Q_WIDTH:QK_WIDTH],
        attn[:, :, QK_WIDTH + Q_WIDTH :],
        attn[:, :, QK_WIDTH : QK_WIDTH + Q_WIDTH],
        last[2 * rows : 4 * rows].reshape(2, rows),
        *feed,
    )


def solution(mesh):
    rows = P(("rep", "fsdp"), None)
    flat, cube = P(None, "fsdp"), P(None, "fsdp", None)
    in_specs = (rows, P(("rep", "fsdp")), flat, cube, cube, cube, cube, flat, cube, cube, cube, rows)
    out_specs = (rows, rows, flat, cube, cube, cube, cube, flat, cube, cube, cube)
    return jax.shard_map(local, mesh=mesh, in_specs=in_specs, out_specs=out_specs, check_vma=False)
```

```python
import functools

import jax
import jax.numpy as jnp
from jax import lax
from jax.experimental import pallas as pl
from jax.experimental.pallas import tpu as pltpu
from jax.sharding import PartitionSpec as P

QUERY_HEADS = 9
KEY_VALUE_HEADS = 3
HEAD_WIDTH = 64
DECODER_LAYERS = 2
MICRO = 2
GROUP = QUERY_HEADS // KEY_VALUE_HEADS
Q_WIDTH = QUERY_HEADS * HEAD_WIDTH
KV_WIDTH = KEY_VALUE_HEADS * HEAD_WIDTH
QK_WIDTH = Q_WIDTH + KV_WIDTH
LSE_ROWS = 16
SCALE = HEAD_WIDTH ** (-0.5)

epsilon = 1e-05
rope_base = 100000.0
masked_fill = -1e30
f32 = jnp.float32
bf16 = jnp.bfloat16


def nn(left, right):
    return jnp.dot(left, right, preferred_element_type=f32)


def nt(left, right):
    return lax.dot_general(left, right, (((1,), (1,)), ((), ())), preferred_element_type=f32)


def tn(left, right):
    return lax.dot_general(left, right, (((0,), (0,)), ((), ())), preferred_element_type=f32)


def swap_halves(rows):
    lane = lax.broadcasted_iota(jnp.int32, rows.shape, 1)
    first = (lane % HEAD_WIDTH) < HEAD_WIDTH // 2
    return jnp.where(
        first, pltpu.roll(rows, 128 - HEAD_WIDTH // 2, 1), pltpu.roll(rows, HEAD_WIDTH // 2, 1)
    )


def rotate(rows, cosine, sine):
    parts = []
    for first in range(0, rows.shape[1], 128):
        slab = rows[:, first : first + 128]
        parts.append(slab * cosine + swap_halves(slab) * sine)
    return jnp.concatenate(parts, axis=1)


def tile_of(rows):
    return 256 if rows % 256 == 0 else rows


def heads_stacked(ref, start, size, group):
    first = group * GROUP * HEAD_WIDTH
    piece = ref[start : start + size, first : first + GROUP * HEAD_WIDTH]
    return jnp.concatenate(
        [piece[:, j * HEAD_WIDTH : (j + 1) * HEAD_WIDTH] for j in range(GROUP)], axis=0
    )


def heads_split(stacked, size):
    turned = stacked.T
    return [turned[j * size : (j + 1) * size] for j in range(GROUP)]


def mask_bias(column_ref, row_ref, start, size):
    reach = start + size
    shape = (reach, size)
    key = lax.broadcasted_iota(jnp.int32, shape, 0)
    query = lax.broadcasted_iota(jnp.int32, shape, 1) + start
    same = column_ref[:reach, :] == row_ref[0, :, start:reach]
    bias = jnp.where(same & (key <= query), 0.0, masked_fill)
    return jnp.concatenate([bias] * GROUP, axis=1)


def norm(rows):
    return lax.rsqrt(jnp.mean(rows * rows, axis=-1, keepdims=True) + epsilon)


def row_line(ref, start, size, group):
    return jnp.concatenate(
        [ref[group * GROUP + j : group * GROUP + j + 1, start : start + size] for j in range(GROUP)],
        axis=1,
    )


MESH_AXES = ("rep", "fsdp")


class Place:
    def __init__(self):
        self.copies = lax.axis_size("rep")
        self.line = lax.axis_size("fsdp") // 2
        self.r = lax.axis_index("rep")
        index = lax.axis_index("fsdp")
        self.z = index // 2
        self.c = index % 2

    def at(self, r, z, c):
        return (r, 2 * z + c)

    def partner(self):
        return self.at(self.r, self.z, 1 - self.c)

    def chip(self, k):
        return lax.rem(self.z + k, self.line)

    def replica(self, j):
        return lax.rem(self.r + j, self.copies)

    def greet(self):
        barrier = pltpu.get_barrier_semaphore()
        peers = [self.partner()]
        peers += [self.at(self.r, self.chip(k), self.c) for k in range(1, self.line)]
        peers += [self.at(self.replica(j), self.z, self.c) for j in range(1, self.copies)]
        for peer in peers:
            pl.semaphore_signal(barrier, inc=1, device_id=peer, device_id_type=pl.DeviceIdType.MESH)
        pl.semaphore_wait(barrier, len(peers))


def remote(source, target, send, receive, device):
    return pltpu.make_async_remote_copy(
        src_ref=source, dst_ref=target, send_sem=send, recv_sem=receive,
        device_id=device, device_id_type=pl.DeviceIdType.MESH,
    )


def part_of(dims, parts):
    rows, cols = dims
    if cols % (128 * parts) == 0:
        return 1, cols // parts
    return 0, rows // parts


def can_cut(dims, parts):
    rows, cols = dims
    return cols % (128 * parts) == 0 or rows % (16 * parts) == 0


def piece(ref, lead, dims, parts, index):
    axis, size = part_of(dims, parts)
    if axis == 1:
        return ref.at[lead, :, pl.ds(pl.multiple_of(index * size, 128), size)]
    return ref.at[lead, pl.ds(pl.multiple_of(index * size, 16), size), :]


def piece_dims(dims, parts):
    axis, size = part_of(dims, parts)
    return (dims[0], size) if axis == 1 else (size, dims[1])


class Gather:
    def __init__(self, place, shard, whole, sems):
        self.p, self.shard, self.whole, self.sems = place, shard, whole, sems
        self.dims = whole.shape[1:]
        self.parts = place.copies

    @staticmethod
    def semaphores(copies, line):
        return [
            pltpu.SemaphoreType.DMA((2, line)),
            pltpu.SemaphoreType.DMA((2, line, copies)),
            pltpu.SemaphoreType.DMA((2, line)),
            pltpu.SemaphoreType.DMA,
        ]

    def own(self):
        p = self.p
        return pltpu.make_async_copy(
            self.shard[0].at[self.shard[1]], self.whole.at[2 * p.z + p.c], self.sems[3]
        )

    def along(self, k):
        p = self.p
        return remote(
            piece(self.shard[0], self.shard[1], self.dims, self.parts, p.r),
            piece(self.whole, 2 * p.z + p.c, self.dims, self.parts, p.r),
            self.sems[0].at[0, k], self.sems[0].at[1, k], p.at(p.r, p.chip(k), p.c),
        )

    def across(self, k, j):
        p = self.p
        block = piece(self.whole, 2 * p.chip(p.line - k) + p.c, self.dims, self.parts, p.r)
        return remote(
            block, block, self.sems[1].at[0, k, j], self.sems[1].at[1, k, j],
            p.at(p.replica(j), p.z, p.c),
        )

    def pair(self, k):
        p = self.p
        block = self.whole.at[2 * p.chip(p.line - k) + p.c]
        return remote(block, block, self.sems[2].at[0, k], self.sems[2].at[1, k], p.partner())

    def others(self):
        return [(k, j) for k in range(1, self.p.line) for j in range(1, self.p.copies)]

    def line_start(self):
        for k in range(1, self.p.line):
            self.along(k).start()
        self.own().start()

    def line_end(self):
        for k in range(1, self.p.line):
            self.along(k).wait_recv()

    def across_start(self):
        for k, j in self.others():
            self.across(k, j).start()

    def across_end(self):
        for k, j in self.others():
            self.across(k, j).wait_recv()

    def pair_start(self):
        for k in range(self.p.line):
            self.pair(k).start()

    def line_done(self):
        self.own().wait()
        for k in range(1, self.p.line):
            self.along(k).wait_send()

    def across_done(self):
        for k, j in self.others():
            self.across(k, j).wait_send()

    def pair_done(self):
        for k in range(self.p.line):
            self.pair(k).wait()


def gathers(place, shards, wholes, sems):
    return [
        Gather(place, shards[i] if shards else None, wholes[i], sems[4 * i : 4 * i + 4])
        for i in range(len(wholes))
    ]


def gather_semaphores(count):
    copies, devices = lax.axis_size("rep"), lax.axis_size("fsdp")
    sems = []
    for _ in range(count):
        sems += Gather.semaphores(copies, devices // 2)
    return sems


class Reduce:
    def __init__(self, place, source, out, buffers, first=0, width=None):
        self.p, self.out, self.first = place, out, first
        self.source = source
        self.dims = (source.shape[1], width or source.shape[2])
        self.parts = place.copies
        (self.mine, self.theirs, self.across_in, self.line_out, self.line_in, self.final,
         self.s0, self.s1, self.s2, self.s3, self.s4) = buffers

    @staticmethod
    def scratch(dims, copies, line):
        small = piece_dims(dims, copies)
        return [
            pltpu.VMEM((line,) + tuple(dims), bf16),
            pltpu.VMEM((line,) + tuple(dims), bf16),
            pltpu.VMEM((copies, line) + small, bf16),
            pltpu.VMEM((line,) + small, bf16),
            pltpu.VMEM((line,) + small, bf16),
            pltpu.VMEM((copies,) + small, bf16),
            pltpu.SemaphoreType.DMA((2, line)),
            pltpu.SemaphoreType.DMA((line,)),
            pltpu.SemaphoreType.DMA((2, copies, line)),
            pltpu.SemaphoreType.DMA((2, line)),
            pltpu.SemaphoreType.DMA((2, copies)),
        ]

    def shard(self, index):
        if self.dims[1] == self.source.shape[2]:
            return self.source.at[index]
        return self.source.at[index, :, pl.ds(self.first, self.dims[1])]

    def pair(self, z):
        p = self.p
        return remote(
            self.shard(2 * z + 1 - p.c), self.theirs.at[z],
            self.s0.at[0, z], self.s0.at[1, z], p.partner(),
        )

    def load(self, z):
        return pltpu.make_async_copy(
            self.shard(2 * z + self.p.c), self.mine.at[z], self.s1.at[z]
        )

    def across(self, j, z):
        p = self.p
        return remote(
            piece(self.mine, z, self.dims, self.parts, p.replica(j)), self.across_in.at[j, z],
            self.s2.at[0, j, z], self.s2.at[1, j, z], p.at(p.replica(j), p.z, p.c),
        )

    def along(self, k):
        p = self.p
        return remote(
            self.line_out.at[p.chip(k)], self.line_in.at[k],
            self.s3.at[0, k], self.s3.at[1, k], p.at(p.r, p.chip(k), p.c),
        )

    def spread(self, j):
        p = self.p
        return remote(
            self.final.at[p.r], self.final.at[p.r],
            self.s4.at[0, j], self.s4.at[1, j], p.at(p.replica(j), p.z, p.c),
        )

    def start(self):
        for z in range(self.p.line):
            self.pair(z).start()
            self.load(z).start()

    def second(self):
        for z in range(self.p.line):
            self.load(z).wait()
            self.pair(z).wait_recv()
            self.mine[z] = (self.mine[z].astype(f32) + self.theirs[z].astype(f32)).astype(bf16)
            for j in range(1, self.p.copies):
                self.across(j, z).start()

    def third(self):
        for z in range(self.p.line):
            total = piece(self.mine, z, self.dims, self.parts, self.p.r)[...].astype(f32)
            for j in range(1, self.p.copies):
                self.across(j, z).wait_recv()
                total += self.across_in[j, z].astype(f32)
            self.line_out[z] = total.astype(bf16)
        for k in range(1, self.p.line):
            self.along(k).start()

    def fourth(self):
        total = self.line_out[self.p.z].astype(f32)
        for k in range(1, self.p.line):
            self.along(k).wait_recv()
            total += self.line_in[k].astype(f32)
        self.final[self.p.r] = total.astype(bf16)
        for j in range(1, self.p.copies):
            self.spread(j).start()

    def finish(self):
        self.write()
        for z in range(self.p.line):
            self.pair(z).wait_send()
            for j in range(1, self.p.copies):
                self.across(j, z).wait_send()
        for k in range(1, self.p.line):
            self.along(k).wait_send()

    def write(self):
        for j in range(1, self.p.copies):
            self.spread(j).wait()
        axis, size = part_of(self.dims, self.parts)
        for index in range(self.parts):
            here = index * size
            if axis == 1:
                here += self.first
                self.out[:, here : here + size] = self.final[index].astype(f32)
            else:
                self.out[here : here + size, :] = self.final[index].astype(f32)


class LineReduce(Reduce):
    @staticmethod
    def scratch(dims, copies, line):
        small = piece_dims(dims, copies)
        return [
            pltpu.VMEM((line,) + tuple(dims), bf16),
            pltpu.VMEM((line,) + tuple(dims), bf16),
            pltpu.VMEM((copies,) + small, bf16),
            pltpu.VMEM((1,) + tuple(dims), bf16),
            pltpu.VMEM((line,) + tuple(dims), bf16),
            pltpu.VMEM((copies,) + small, bf16),
            pltpu.SemaphoreType.DMA((2, line)),
            pltpu.SemaphoreType.DMA((line,)),
            pltpu.SemaphoreType.DMA((2, copies)),
            pltpu.SemaphoreType.DMA((2, line)),
            pltpu.SemaphoreType.DMA((2, copies)),
        ]

    def along(self, k):
        p = self.p
        return remote(
            self.mine.at[p.chip(k)], self.line_in.at[k],
            self.s3.at[0, k], self.s3.at[1, k], p.at(p.r, p.chip(k), p.c),
        )

    def across(self, j):
        p = self.p
        return remote(
            piece(self.line_out, 0, self.dims, self.parts, p.replica(j)), self.across_in.at[j],
            self.s2.at[0, j], self.s2.at[1, j], p.at(p.replica(j), p.z, p.c),
        )

    def second(self):
        for z in range(self.p.line):
            self.load(z).wait()
            self.pair(z).wait_recv()
            self.mine[z] = (self.mine[z].astype(f32) + self.theirs[z].astype(f32)).astype(bf16)
        for k in range(1, self.p.line):
            self.along(k).start()

    def third(self):
        total = self.mine[self.p.z].astype(f32)
        for k in range(1, self.p.line):
            self.along(k).wait_recv()
            total += self.line_in[k].astype(f32)
        self.line_out[0] = total.astype(bf16)
        for j in range(1, self.p.copies):
            self.across(j).start()

    def fourth(self):
        total = piece(self.line_out, 0, self.dims, self.parts, self.p.r)[...].astype(f32)
        for j in range(1, self.p.copies):
            self.across(j).wait_recv()
            total += self.across_in[j].astype(f32)
        self.final[self.p.r] = total.astype(bf16)
        for j in range(1, self.p.copies):
            self.spread(j).start()

    def finish(self):
        self.write()
        for z in range(self.p.line):
            self.pair(z).wait_send()
        for k in range(1, self.p.line):
            self.along(k).wait_send()
        for j in range(1, self.p.copies):
            self.across(j).wait_send()


def kinds_of(count):
    return [Reduce, Reduce, LineReduce][:count]


def reduce_buffers(sources):
    copies, devices = lax.axis_size("rep"), lax.axis_size("fsdp")
    buffers = []
    for kind, g in zip(kinds_of(len(sources)), sources):
        buffers += kind.scratch(g.shape[1:], copies, devices // 2)
    return buffers


def reduces(place, sources, results, buffers):
    return [
        kind(place, sources[i], results[i], buffers[11 * i : 11 * i + 11])
        for i, kind in enumerate(kinds_of(len(sources)))
    ]


class Plan:
    def __init__(self, step, steps):
        self.step, self.steps, self.at = step, steps, {}

    def put(self, when, point, *acts):
        self.at.setdefault((when, point), []).extend(acts)

    def run(self, point):
        for when in range(self.steps):
            acts = self.at.get((when, point), [])
            if acts:
                @pl.when(self.step == when)
                def _(acts=acts):
                    for act in acts:
                        act()


def feed_line(plan, points, moves):
    gate, up, down = moves
    (one, two), last = points[0], points[1]
    plan.put(one, two, gate.line_end, gate.across_start, up.line_start, down.line_start)
    plan.put(*last, up.line_end, down.line_end, gate.across_end, gate.across_done)
    plan.put(*last, *[move.line_done for move in moves])


def prepare_kernel(counts, column_ref, row_ref, frequency_ref, *refs):
    attn_count, feed_count = counts
    total = attn_count + feed_count
    shards, refs = refs[:total], refs[total:]
    live_ref, table_ref, *refs = refs
    wholes, sems = refs[:total], refs[total:]
    if total:
        place = Place()
        moves = gathers(place, [(ref, 0) for ref in shards], wholes, sems)
        first, feed = moves[:attn_count], moves[attn_count:]
        place.greet()
        for move in first:
            move.line_start()
    size = row_ref.shape[2]
    live_ref[...] = jnp.where(column_ref[...] >= 0, 1.0, 0.0).astype(f32)
    key = lax.broadcasted_iota(jnp.int32, (size, size), 1)
    query = lax.broadcasted_iota(jnp.int32, (size, size), 0)
    positions = []
    for block in range(MICRO):
        same = column_ref[block * size : (block + 1) * size, :] == row_ref[block]
        earlier = jnp.where(same & (key < query), 1.0, 0.0)
        positions.append(jnp.sum(earlier, axis=1, keepdims=True))
    if total:
        for move in first:
            move.line_end()
            move.across_start()
        feed[0].line_start()
    lane = lax.broadcasted_iota(jnp.int32, (size, 128), 1)
    sign = jnp.where(lane % HEAD_WIDTH < HEAD_WIDTH // 2, -1.0, 1.0)
    for block in range(MICRO):
        angles = positions[block] * frequency_ref[...]
        here = slice(block * size, (block + 1) * size)
        table_ref[here, :128] = jnp.cos(angles)
        table_ref[here, 128:] = jnp.sin(angles) * sign
    if total:
        gate = feed[0]
        gate.line_end()
        gate.across_start()
        for move in feed[1:]:
            move.line_start()
        for move in first:
            move.across_end()
            move.own().wait()
            move.pair_start()
        for move in feed[1:]:
            move.line_end()
        gate.across_end()
        gate.across_done()
        for move in feed:
            move.line_done()
        for move in first:
            for k in range(1, place.line):
                move.along(k).wait_send()
            move.across_done()
            move.pair_done()


def prepare(segment, shards=(), feed=(), collective_id=None):
    rows = segment.shape[0]
    size = rows // MICRO
    devices = lax.axis_size("fsdp")
    frequency = rope_base ** (-2.0 * jnp.arange(HEAD_WIDTH // 2, dtype=f32) / HEAD_WIDTH)
    frequency = jnp.concatenate([frequency] * 4)[None]
    everything = tuple(shards) + tuple(feed)
    wholes = [shape((devices,) + w.shape[1:], bf16) for w in everything]
    vmem = pl.BlockSpec(memory_space=pltpu.VMEM)
    extra = {}
    if everything:
        extra = {"collective_id": collective_id, "has_side_effects": True}
    return pl.pallas_call(
        functools.partial(prepare_kernel, (len(shards), len(feed))),
        in_specs=[vmem] * 3 + [any_spec() for _ in everything],
        out_specs=[vmem] * 2 + [any_spec() for _ in everything],
        out_shape=[shape((rows, 1), f32), shape((rows, 256), f32)] + wholes,
        scratch_shapes=gather_semaphores(len(everything)),
        compiler_params=pltpu.CompilerParams(vmem_limit_bytes=62 * 2**20, **extra),
        name="prepare",
    )(segment.reshape(-1, 1), segment.reshape(MICRO, 1, size), frequency, *everything)


def attn_forward_kernel(
    row, count, turned, x_ref, column_ref, row_ref, live_ref, table_ref, gain_ref, weight_ref,
    *rest
):
    h_ref, qk_ref, v_ref, a_ref, lse_ref, *rest = rest[count:]
    wholes, sems = rest[:count], rest[count:]
    plan = Plan(pl.program_id(0), MICRO)
    if count:
        place = Place()
        gate, up, down = gathers(place, (), wholes, sems)
        plan.put(0, "start", place.greet, up.across_start, gate.pair_start)
        plan.put(0, 7, down.across_start)
        plan.put(0, "end", up.across_end, up.pair_start)
        plan.put(1, 7, down.across_end, down.pair_start)
        plan.put(1, "end", gate.pair_done, up.across_done, up.pair_done)
        plan.put(1, "end", down.across_done, down.pair_done)
    plan.run("start")
    x = (x_ref[...].T if turned else x_ref[...]).astype(f32)
    rows = x.shape[0]
    h_ref[...] = x
    normed = (x * norm(x) * gain_ref[row : row + 1, :]).astype(bf16)
    qk = nn(normed, weight_ref[:, :QK_WIDTH])
    v_ref[...] = nn(normed, weight_ref[:, QK_WIDTH + Q_WIDTH :]).astype(bf16)
    qk = rotate(qk, table_ref[:, :128], table_ref[:, 128:]).astype(bf16)
    qk_ref[:, :Q_WIDTH] = qk[:, :Q_WIDTH] * SCALE
    qk_ref[:, Q_WIDTH:] = qk[:, Q_WIDTH:]
    size = tile_of(rows)
    tiles = rows // size
    for tile in range(tiles):
        start = tile * size
        reach = start + size
        bias = mask_bias(column_ref, row_ref, start, size)
        outputs = []
        for group in range(KEY_VALUE_HEADS):
            lanes = slice(group * HEAD_WIDTH, (group + 1) * HEAD_WIDTH)
            klanes = slice(Q_WIDTH + group * HEAD_WIDTH, Q_WIDTH + (group + 1) * HEAD_WIDTH)
            queries = heads_stacked(qk_ref, start, size, group)
            scores = nt(qk_ref[:reach, klanes], queries) + bias
            peak = jnp.max(scores, axis=0, keepdims=True)
            expo = jnp.exp(scores - peak)
            total = jnp.sum(expo, axis=0, keepdims=True)
            mixed = tn(v_ref[:reach, lanes], expo.astype(bf16)) * (1.0 / total)
            outputs += heads_split(mixed, size)
            line = peak + jnp.log(total)
            for j in range(GROUP):
                lse_ref[group * GROUP + j : group * GROUP + j + 1, start:reach] = line[
                    :, j * size : (j + 1) * size
                ]
            plan.run(tile * KEY_VALUE_HEADS + group)
        a_ref[start:reach, :] = jnp.concatenate(outputs, axis=1).astype(bf16)
    out = nn(a_ref[...], weight_ref[:, QK_WIDTH : QK_WIDTH + Q_WIDTH])
    h_ref[...] = h_ref[...] + out * live_ref[...]
    for point in range(tiles * KEY_VALUE_HEADS, 9):
        plan.run(point)
    plan.run("end")


def attn_backward_kernel(
    row, count, turned, x_ref, dh_ref, column_ref, row_ref, live_ref, table_ref, gain_ref, weight_ref,
    qk_ref, v_ref, a_ref, lse_ref, *rest
):
    sources, rest = rest[:count], rest[count:]
    dx_ref, grad_ref, gain_grad_ref, *rest = rest
    results, rest = rest[:count], rest[count:]
    (n1t_ref, at_ref, c_ref, dqk_ref, dv_ref, da_ref, weight_line_ref, dqk_sum, dv_sum) = rest[:9]
    buffers = rest[9:]
    step = pl.program_id(0)
    plan = Plan(step, MICRO)
    if count:
        place = Place()
        moves = reduces(place, sources, results, buffers)
        plan.put(0, "start", place.greet, *[move.start for move in moves])
        one, two = moves[:2]
        plan.put(0, 0, one.second)
        plan.put(0, 4, two.second)
        plan.put(0, 8, one.third)
        plan.put(1, 2, two.third)
        if count == 3:
            plan.put(0, 0, moves[2].second)
            plan.put(1, 3, one.fourth)
            plan.put(1, 4, moves[2].third)
            plan.put(1, 7, moves[2].fourth)
        else:
            plan.put(1, 1, one.fourth)
        plan.put(1, "grads", two.fourth)
        plan.put(1, "end", *[move.finish for move in moves])
    plan.run("start")
    rows = dh_ref.shape[0]
    here = pl.ds(pl.multiple_of(step * rows, rows), rows)
    c = (dh_ref[...] * live_ref[...]).astype(bf16)
    c_ref[here, :] = c
    da = nt(c, weight_ref[:, QK_WIDTH : QK_WIDTH + Q_WIDTH]).astype(bf16)
    da_ref[...] = da
    a = a_ref[...]
    at_ref[:, here] = a.T
    product = da.astype(f32) * a.astype(f32)
    high = product.astype(bf16)
    low = (product - high.astype(f32)).astype(bf16)
    pick = (
        lax.broadcasted_iota(jnp.int32, (LSE_ROWS, Q_WIDTH), 1) // HEAD_WIDTH
        == lax.broadcasted_iota(jnp.int32, (LSE_ROWS, Q_WIDTH), 0)
    )
    pick = jnp.where(pick, 1.0, 0.0).astype(bf16)
    weight_line_ref[...] = nt(pick, high) + nt(pick, low)
    size = tile_of(rows)
    tiles = rows // size
    for tile in reversed(range(tiles)):
        start = tile * size
        reach = start + size
        bias = mask_bias(column_ref, row_ref, start, size)
        query_grads = []
        for group in range(KEY_VALUE_HEADS):
            lanes = slice(group * HEAD_WIDTH, (group + 1) * HEAD_WIDTH)
            klanes = slice(Q_WIDTH + group * HEAD_WIDTH, Q_WIDTH + (group + 1) * HEAD_WIDTH)
            queries = heads_stacked(qk_ref, start, size, group)
            upstream = heads_stacked(da_ref, start, size, group)
            keys = qk_ref[:reach, klanes]
            values = v_ref[:reach, lanes]
            probs = jnp.exp(nt(keys, queries) + bias - row_line(lse_ref, start, size, group))
            value_grad = nn(probs.astype(bf16), upstream)
            grad_probs = nt(values, upstream)
            grad_scores = (
                probs * (grad_probs - row_line(weight_line_ref, start, size, group))
            ).astype(bf16)
            key_grad = nn(grad_scores, queries)
            query_grads += heads_split(tn(keys, grad_scores) * SCALE, size)
            if reach == rows:
                dqk_sum[:, klanes] = key_grad
                dv_sum[:, lanes] = value_grad
            else:
                dqk_sum[:reach, klanes] += key_grad
                dv_sum[:reach, lanes] += value_grad
            plan.run((tiles - 1 - tile) * KEY_VALUE_HEADS + group)
        dqk_sum[start:reach, :Q_WIDTH] = jnp.concatenate(query_grads, axis=1)
    for point in range(tiles * KEY_VALUE_HEADS, 9):
        plan.run(point)
    dqk = rotate(dqk_sum[...], table_ref[:, :128], -table_ref[:, 128:]).astype(bf16)
    dqk_ref[here, :] = dqk
    dv = dv_sum[...].astype(bf16)
    dv_ref[here, :] = dv
    dn = nt(dqk, weight_ref[:, :QK_WIDTH]) + nt(dv, weight_ref[:, QK_WIDTH + Q_WIDTH :])
    x = (x_ref[...].T if turned else x_ref[...]).astype(f32)
    factor = norm(x)
    unit = x * factor
    gain = gain_ref[row : row + 1, :]
    n1t_ref[:, here] = (unit * gain).astype(bf16).T
    scaled = dn * gain
    dx = dh_ref[...] + factor * (
        scaled - unit * jnp.mean(scaled * unit, axis=-1, keepdims=True)
    )
    dx_ref[...] = dx.T if turned else dx
    gain_part = jnp.sum(dn * unit, axis=0, keepdims=True)

    @pl.when(step == 0)
    def _():
        gain_grad_ref[...] = gain_part

    @pl.when(step > 0)
    def _():
        gain_grad_ref[...] += gain_part

    plan.run("grads")

    @pl.when(step == pl.num_programs(0) - 1)
    def _():
        grad_ref[:, :QK_WIDTH] = nn(n1t_ref[...], dqk_ref[...]).astype(bf16)
        grad_ref[:, QK_WIDTH : QK_WIDTH + Q_WIDTH] = nn(at_ref[...], c_ref[...]).astype(bf16)
        grad_ref[:, QK_WIDTH + Q_WIDTH :] = nn(n1t_ref[...], dv_ref[...]).astype(bf16)

    plan.run("end")


def ff_forward_kernel(
    row, layer, count, steps, h_ref, live_ref, gain_ref, wg_ref, wu_ref, wd_ref, *rest
):
    shards, (y_ref, *rest) = rest[:count], rest[count:]
    wholes, sems = rest[:count], rest[count:]
    plan = Plan(pl.program_id(0), steps)
    if count:
        place = Place()
        moves = gathers(place, [(ref, layer) for ref in shards], wholes, sems)
        plan.put(0, "start", place.greet, moves[0].line_start)
        feed_line(plan, ((steps * 2 // 6, "end"), (steps - 1, "end")), moves)
    plan.run("start")
    h = h_ref[...]
    normed = (h * norm(h) * gain_ref[row : row + 1, :]).astype(bf16)
    gate = nn(normed, wg_ref[...])
    up = nn(normed, wu_ref[...])
    half = 0.5 * gate
    inner = ((half + half * jnp.tanh(half)) * up).astype(bf16)
    y_ref[...] = h + nn(inner, wd_ref[...]) * live_ref[...]
    plan.run("end")


def ff_backward_kernel(
    row, last, count, steps, h_ref, dy_ref, live_ref, gain_ref, wg_ref, wu_ref, wd_ref, *rest,
):
    sources, rest = rest[:count], rest[count:]
    if last:
        y_ref, *rest = rest
    dh_ref, gg_ref, gu_ref, gd_ref, gain_grad_ref, *rest = rest
    results, rest = rest[:count], rest[count:]
    n2t_ref, et_ref, m_ref, dg_ref, du_ref, *buffers = rest
    step = pl.program_id(0)
    plan = Plan(step, steps)
    if count:
        place = Place()
        one, two = reduces(place, sources, results, buffers)
        plan.put(0, "start", place.greet, one.start, two.start)
        plan.put(0, "middle", one.second)
        plan.put(steps * 2 // 6, "middle", two.second)
        plan.put(steps * 3 // 6, "middle", one.third)
        plan.put(steps * 4 // 6, "end", one.fourth, two.third)
        plan.put(steps - 1, "half", two.fourth)
        plan.put(steps - 1, "last", one.finish, two.finish)
    plan.run("start")
    rows = h_ref.shape[0]
    here = pl.ds(pl.multiple_of(step * rows, rows), rows)
    h = h_ref[...]
    factor = norm(h)
    unit = h * factor
    gain = gain_ref[row : row + 1, :]
    normed = (unit * gain).astype(bf16)
    n2t_ref[:, here] = normed.T
    live = live_ref[...]
    dy = (dy_ref[...].T if last else dy_ref[...]).astype(f32)
    e = (dy * live).astype(bf16)
    et_ref[:, here] = e.T
    gate = nn(normed, wg_ref[...])
    up = nn(normed, wu_ref[...])
    sig = 0.5 + 0.5 * jnp.tanh(0.5 * gate)
    silu = gate * sig
    inner = (silu * up).astype(bf16)
    m_ref[here, :] = inner
    plan.run("middle")
    dm = nt(e, wd_ref[...]).astype(bf16).astype(f32)
    dgate = (dm * up * (sig + silu * (1.0 - sig))).astype(bf16)
    dup = (dm * silu).astype(bf16)
    dg_ref[here, :] = dgate
    du_ref[here, :] = dup
    if last:
        y_ref[...] = (h + nn(inner, wd_ref[...]) * live).astype(bf16).T
    dn = nt(dgate, wg_ref[...]) + nt(dup, wu_ref[...])
    scaled = dn * gain
    dh_ref[...] = dy + factor * (scaled - unit * jnp.mean(scaled * unit, axis=-1, keepdims=True))
    gain_part = jnp.sum(dn * unit, axis=0, keepdims=True)

    plan.run("end")

    @pl.when(step == 0)
    def _():
        gain_grad_ref[...] = gain_part

    @pl.when(step > 0)
    def _():
        gain_grad_ref[...] += gain_part

    def weight_grads(first):
        cols = slice(first, first + 512)
        gg_ref[:, cols] = nn(n2t_ref[...], dg_ref[:, cols]).astype(bf16)
        gu_ref[:, cols] = nn(n2t_ref[...], du_ref[:, cols]).astype(bf16)
        gd_ref[cols, :] = nn(et_ref[...], m_ref[:, cols]).astype(bf16).T

    ff = m_ref.shape[1]

    @pl.when(step == steps - 1)
    def _():
        weight_grads(0)

    plan.run("half")

    @pl.when(step == steps - 1)
    def _():
        for first in range(512, ff, 512):
            weight_grads(first)

    plan.run("last")


def row_spec(size, width):
    return pl.BlockSpec((size, width), lambda i: (i, 0))


def whole_spec(shape):
    return pl.BlockSpec(shape, lambda i: (0,) * len(shape), pipeline_mode=pl.Buffered(1))


def turned_spec(size, width):
    return pl.BlockSpec((width, size), lambda i: (0, i))


def still_spec(shape):
    return pl.BlockSpec(shape, lambda i: (0,) * len(shape))


def shape(dims, dtype):
    return jax.ShapeDtypeStruct(dims, dtype)


def params(collective_id=None, mib=62):
    extra = {}
    if collective_id is not None:
        extra = {"collective_id": collective_id, "has_side_effects": True}
    return pltpu.CompilerParams(
        vmem_limit_bytes=mib * 2**20, dimension_semantics=("arbitrary",), **extra
    )


def any_spec():
    return pl.BlockSpec(memory_space=pl.ANY)


def cost(flops, *arrays):
    return pl.CostEstimate(
        flops=int(flops),
        bytes_accessed=sum(int(a.size) * a.dtype.itemsize for a in arrays),
        transcendentals=0,
    )


def attn_forward(
    x, segment, live, table, gain, weight, row, turned, collective_id=None, halves=()
):
    total, width = x.shape[::-1] if turned else x.shape
    size = total // MICRO
    outs = [
        shape((total, width), f32),
        shape((total, QK_WIDTH), bf16),
        shape((total, KV_WIDTH), bf16),
        shape((total, Q_WIDTH), bf16),
        shape((LSE_ROWS, total), f32),
    ]
    return pl.pallas_call(
        functools.partial(attn_forward_kernel, row, len(halves), turned),
        grid=(MICRO,),
        in_specs=[
            turned_spec(size, width) if turned else row_spec(size, width),
            row_spec(size, 1),
            pl.BlockSpec((1, 1, size), lambda i: (i, 0, 0)),
            row_spec(size, 1),
            row_spec(size, 256),
            whole_spec(gain.shape),
            whole_spec(weight.shape),
        ]
        + [any_spec() for _ in halves],
        out_specs=[row_spec(size, o.shape[1]) for o in outs[:4]]
        + [pl.BlockSpec((LSE_ROWS, size), lambda i: (0, i))]
        + [any_spec() for _ in halves],
        out_shape=outs + [shape(w.shape, bf16) for w in halves],
        scratch_shapes=gather_semaphores(len(halves)),
        input_output_aliases={7 + k: 5 + k for k in range(len(halves))},
        compiler_params=params(collective_id),
        cost_estimate=cost(2 * total * (width * 1536 + size * Q_WIDTH * 4), x, weight, *outs),
        name="attn_fwd",
    )(x, segment.reshape(-1, 1), segment.reshape(MICRO, 1, size), live, table, gain, weight, *halves)


def attn_backward(
    x, dh, segment, live, table, gain, weight, saved, row, turned, collective_id=None, sources=()
):
    total, width = dh.shape
    sums = [shape(g.shape[1:], f32) for g in sources]
    buffers = reduce_buffers(sources)
    size = total // MICRO
    qk, v, a, lse = saved
    outs = [shape(x.shape, f32), shape(weight.shape, bf16), shape((1, width), f32)]
    x_spec = turned_spec(size, width) if turned else row_spec(size, width)
    return pl.pallas_call(
        functools.partial(attn_backward_kernel, row, len(sources), turned),
        grid=(MICRO,),
        in_specs=[
            x_spec,
            row_spec(size, width),
            row_spec(size, 1),
            pl.BlockSpec((1, 1, size), lambda i: (i, 0, 0)),
            row_spec(size, 1),
            row_spec(size, 256),
            whole_spec(gain.shape),
            whole_spec(weight.shape),
            row_spec(size, QK_WIDTH),
            row_spec(size, KV_WIDTH),
            row_spec(size, Q_WIDTH),
            pl.BlockSpec((LSE_ROWS, size), lambda i: (0, i)),
        ]
        + [any_spec() for _ in sources],
        out_specs=[x_spec, whole_spec(weight.shape), still_spec((1, width))]
        + [whole_spec(o.shape) for o in sums],
        out_shape=outs + sums,
        scratch_shapes=[
            pltpu.VMEM((width, total), bf16),
            pltpu.VMEM((Q_WIDTH, total), bf16),
            pltpu.VMEM((total, width), bf16),
            pltpu.VMEM((total, QK_WIDTH), bf16),
            pltpu.VMEM((total, KV_WIDTH), bf16),
            pltpu.VMEM((size, Q_WIDTH), bf16),
            pltpu.VMEM((LSE_ROWS, size), f32),
            pltpu.VMEM((size, QK_WIDTH), f32),
            pltpu.VMEM((size, KV_WIDTH), f32),
        ]
        + buffers,
        compiler_params=params(collective_id),
        cost_estimate=cost(2 * total * (width * 3072 + size * Q_WIDTH * 10), x, dh, weight, *outs),
        name="attn_bwd",
    )(
        x, dh, segment.reshape(-1, 1), segment.reshape(MICRO, 1, size), live, table, gain, weight,
        qk, v, a, lse, *sources,
    )


CHUNK = 512


def windows(sources):
    return [(i, first) for i, g in enumerate(sources) for first in range(0, g.shape[2], CHUNK)]


def reduce_kernel(count, *refs):
    sources, results, buffers = refs[:count], refs[count : 2 * count], refs[2 * count :]
    place = Place()
    moves = [
        Reduce(place, sources[i], results[i], buffers[11 * n : 11 * n + 11], first, CHUNK)
        for n, (i, first) in enumerate(windows(sources))
    ]
    place.greet()
    for stage in ("start", "second", "third", "fourth", "finish"):
        for move in moves:
            getattr(move, stage)()


def reduce_alone(collective_id, *sources):
    copies, devices = lax.axis_size("rep"), lax.axis_size("fsdp")
    buffers = []
    for i, _ in windows(sources):
        buffers += Reduce.scratch((sources[i].shape[1], CHUNK), copies, devices // 2)
    return pl.pallas_call(
        functools.partial(reduce_kernel, len(sources)),
        in_specs=[any_spec() for _ in sources],
        out_specs=[pl.BlockSpec(memory_space=pltpu.VMEM) for _ in sources],
        out_shape=[shape(g.shape[1:], f32) for g in sources],
        scratch_shapes=buffers,
        compiler_params=pltpu.CompilerParams(
            vmem_limit_bytes=32 * 2**20, collective_id=collective_id, has_side_effects=True
        ),
        name="reduce",
    )(*sources)


def ff_forward(h, live, gain, wg, wu, wd, row, collective_id=None, layer=None, shards=()):
    total, width = h.shape
    devices = lax.axis_size("fsdp")
    wholes = [shape((devices,) + w.shape[1:], bf16) for w in shards]
    size = tile_of(total)
    out = shape((total, width), f32)
    return pl.pallas_call(
        functools.partial(ff_forward_kernel, row, layer, len(shards), total // size),
        grid=(total // size,),
        in_specs=[row_spec(size, width), row_spec(size, 1), whole_spec(gain.shape)]
        + [whole_spec(w.shape) for w in (wg, wu, wd)]
        + [any_spec() for _ in shards],
        out_specs=[row_spec(size, width)] + [any_spec() for _ in shards],
        out_shape=[out] + wholes,
        scratch_shapes=gather_semaphores(len(shards)),
        compiler_params=params(collective_id),
        cost_estimate=cost(6 * total * wg.size, h, wg, wu, wd, out),
        name="ff_fwd",
    )(h, live, gain, wg, wu, wd, *shards)


def ff_backward(h, dy, live, gain, wg, wu, wd, row, last, collective_id=None, sources=()):
    total, width = h.shape
    ff = wg.shape[1]
    size = tile_of(total)
    outs = [
        shape((total, width), f32),
        shape(wg.shape, bf16),
        shape(wu.shape, bf16),
        shape(wd.shape, bf16),
        shape((1, width), f32),
    ]
    sums = [shape(g.shape[1:], f32) for g in sources]
    buffers = reduce_buffers(sources)
    outs += sums
    specs = [row_spec(size, width)] + [whole_spec(o.shape) for o in outs[1:]]
    dy_spec = row_spec(size, width)
    if last:
        outs = [shape((width, total), bf16)] + outs
        dy_spec = turned_spec(size, width)
        specs = [dy_spec] + specs
    return pl.pallas_call(
        functools.partial(ff_backward_kernel, row, last, len(sources), total // size),
        grid=(total // size,),
        in_specs=[row_spec(size, width), dy_spec, row_spec(size, 1)]
        + [whole_spec(gain.shape)]
        + [whole_spec(w.shape) for w in (wg, wu, wd)]
        + [any_spec() for _ in sources],
        out_specs=specs,
        out_shape=outs,
        scratch_shapes=[
            pltpu.VMEM((width, total), bf16),
            pltpu.VMEM((width, total), bf16),
            pltpu.VMEM((total, ff), bf16),
            pltpu.VMEM((total, ff), bf16),
            pltpu.VMEM((total, ff), bf16),
        ]
        + buffers,
        compiler_params=params(collective_id),
        cost_estimate=cost(16 * total * wg.size, h, dy, wg, wu, wd, *outs),
        name="ff_bwd",
    )(h, dy, live, gain, wg, wu, wd, *sources)


def sum_shards(buffer):
    shard = lax.psum_scatter(buffer, "fsdp", scatter_dimension=0, tiled=False)
    return lax.psum(shard, "rep").astype(f32)


def local(
    tokens, segment, attn_gain, w_query, key_weight, value_weight, w_out, mlp_gain,
    gate_weight, up_weight, down_weight, cotangent,
):
    devices = lax.axis_size("fsdp")
    rows, ff = gate_weight.shape[1:]
    width = rows * devices
    down_rows = down_weight.shape[1]
    copies = lax.axis_size("rep")
    shards = (gate_weight, up_weight, down_weight)
    packed_gains = jnp.concatenate([attn_gain, mlp_gain]).reshape(1, 4 * rows)
    room = CHUNK * -(-4 * rows // CHUNK)
    packed_gains = jnp.pad(packed_gains, ((0, 15), (0, room - 4 * rows)))[None]
    packed = [
        jnp.concatenate([w_query[i], key_weight[i], w_out[i], value_weight[i]], axis=1)[None]
        for i in range(DECODER_LAYERS)
    ]
    direct = all(can_cut(w.shape[1:], copies) for w in shards) and can_cut((16, CHUNK), copies)

    def whole(shard):
        return lax.all_gather(shard, "fsdp", axis=0, tiled=True)

    def feed_of(gathered):
        gate, up, down = gathered
        return gate.reshape(width, ff), up.reshape(width, ff), down.reshape(ff, width)

    def split(grads):
        dims = ((rows, ff), (rows, ff), (down_rows, width))
        return [g.reshape((devices,) + d) for g, d in zip(grads, dims)]

    tokens, cotangent = tokens.T, cotangent.T
    if direct:
        live, table, weight0, gains, *feed0 = prepare(
            segment, (packed[0], packed_gains), shards, 0
        )
        packed[1], live = lax.optimization_barrier((packed[1], live))
    else:
        live, table = prepare(segment)
        weight0, gains = whole(packed[0]), whole(packed_gains)
    attn_w = [weight0.reshape(width, ff), whole(packed[1]).reshape(width, ff)]
    gains = gains[:, 0, : 4 * rows].reshape(devices, 4, rows)
    gains = gains.transpose(1, 0, 2).reshape(4, width).astype(f32)
    args0 = (tokens, segment, live, table, gains, attn_w[0], 0, True)
    if direct:
        h0, *kept0 = attn_forward(*args0, 1, feed0)
        kept0, feed0 = kept0[:4], feed_of(kept0[4:])
        x1, *feed1 = ff_forward(h0, live, gains, *feed0, 2, 2, 1, shards)
    else:
        h0, *kept0 = attn_forward(*args0)
        feed0 = feed_of([whole(w[0]) for w in shards])
        x1 = ff_forward(h0, live, gains, *feed0, 2)[0]
    args1 = (x1, segment, live, table, gains, attn_w[1], 1, False)
    if direct:
        h1, *kept1 = attn_forward(*args1, 3, feed1)
        kept1, feed1 = kept1[:4], feed_of(kept1[4:])
    else:
        h1, *kept1 = attn_forward(*args1)
        feed1 = feed_of([whole(w[1]) for w in shards])
    out_tokens, dh1, gg1, gu1, gd1, mg1 = ff_backward(
        h1, cotangent, live, gains, *feed1, 3, True
    )
    grads1 = split((gg1, gu1, gd1))
    args1 = (x1, dh1, segment, live, table, gains, attn_w[1], kept1, 1, False)
    if direct:
        dx1, ga1, ag1, *sums1 = attn_backward(*args1, 4, grads1[:2])
    else:
        dx1, ga1, ag1 = attn_backward(*args1)
    ga1 = ga1.reshape(devices, rows, ff)
    args0 = (h0, dx1, live, gains, *feed0, 2, False)
    if direct:
        dh0, gg0, gu0, gd0, mg0, down1, attn1 = ff_backward(*args0, 5, (grads1[2], ga1))
        sums1.append(down1)
    else:
        sums1, attn1 = [sum_shards(g) for g in grads1], sum_shards(ga1)
        dh0, gg0, gu0, gd0, mg0 = ff_backward(*args0)
    grads0 = split((gg0, gu0, gd0))
    args0 = (tokens, dh0, segment, live, table, gains, attn_w[0], kept0, 0, True)
    if direct:
        dx0, ga0, ag0, *sums0 = attn_backward(*args0, 6, grads0)
    else:
        dx0, ga0, ag0 = attn_backward(*args0)
        sums0 = [sum_shards(g) for g in grads0]
    ga0 = ga0.reshape(devices, rows, ff)
    gain_grads = jnp.concatenate(
        [g.reshape(devices, 1, rows).astype(bf16) for g in (ag0, ag1, mg0, mg1)], axis=2
    )
    gain_grads = jnp.pad(gain_grads, ((0, 0), (0, 15), (0, room - 4 * rows)))
    if direct:
        attn0, last = reduce_alone(7, ga0, gain_grads)
    else:
        attn0, last = sum_shards(ga0), sum_shards(gain_grads)
    last = last[0]
    attn = jnp.stack([attn0, attn1])
    feed = [jnp.stack(pair) for pair in zip(sums0, sums1)]
    return (
        out_tokens.T,
        dx0.T,
        last[: 2 * rows].reshape(2, rows),
        attn[:, :, :Q_WIDTH],
        attn[:, :, Q_WIDTH:QK_WIDTH],
        attn[:, :, QK_WIDTH + Q_WIDTH :],
        attn[:, :, QK_WIDTH : QK_WIDTH + Q_WIDTH],
        last[2 * rows : 4 * rows].reshape(2, rows),
        *feed,
    )


def solution(mesh):
    rows = P(("rep", "fsdp"), None)
    flat, cube = P(None, "fsdp"), P(None, "fsdp", None)
    in_specs = (rows, P(("rep", "fsdp")), flat, cube, cube, cube, cube, flat, cube, cube, cube, rows)
    out_specs = (rows, rows, flat, cube, cube, cube, cube, flat, cube, cube, cube)
    return jax.shard_map(local, mesh=mesh, in_specs=in_specs, out_specs=out_specs, check_vma=False)
```
